256 devices in a mesh: ctx: 32 (over z, y_hi, core), tp: 8 (over x, y_lo).
Axes of the slice: x: 4, y: 4 (y_hi: 2, y_lo: 2; y = y_hi * 2 + y_lo), z: 8, core: 2. Of those that a mesh axis runs over, the one named last changes fastest.
Arguments:
- query_act: bfloat16 [16384, 4096], P('ctx', 'tp'), may hold values from -6 to 6
- key_act: bfloat16 [16384, 4096], P('ctx', 'tp'), may hold values from -6 to 6
- value_act: bfloat16 [16384, 4096], P('ctx', 'tp'), may hold values from -6 to 6
- filters: float32 [128, 4096], P(None, 'tp'), may hold values from -1.25 to 1.25
- out_weight: bfloat16 [4096, 4096], P('ctx', 'tp'), may hold values from -0.09375 to 0.09375
- grad_out: bfloat16 [16384, 4096], P('ctx', 'tp'), may hold values from -6 to 6
Outputs:
- grad_query: bfloat16 [16384, 4096], P('ctx', 'tp')
- grad_key: bfloat16 [16384, 4096], P('ctx', 'tp')
- grad_value: bfloat16 [16384, 4096], P('ctx', 'tp')
- grad_filters: float32 [128, 4096], P(None, 'tp')
- grad_weight: bfloat16 [4096, 4096], P('ctx', 'tp')
The draws below stay inside these ranges and needn't reach their ends.
All inputs are finite; a program needn't handle non-finite values.
Results may differ from the reference program's by a relative error of at most 0.0058.
Values may be sent and summed in bfloat16 or wider, within the bound.
A program may use at most 128 MiB of HBM per device.

```python
import jax
import jax.numpy as jnp
from jax import lax

D = 4096
TAPS = 128
TOKENS = 16384
N_CTX = 32


def draw_filters(key, part):
    key = jax.random.fold_in(key, 7)
    first, second = jax.random.split(key)
    steps = jnp.arange(TAPS, dtype=jnp.float32)[:, None]
    spans = jnp.exp(jax.random.uniform(first, (1, D), jnp.float32, jnp.log(20.0), jnp.log(400.0)))
    noise = jnp.clip(jax.random.normal(second, (TAPS, D), jnp.float32), -4.0, 4.0)
    scale = 1.0 / jnp.sqrt(jnp.minimum(spans, 128.0) * 0.5 + 1.0)
    return (noise * jnp.exp(-steps / spans) * scale).astype(jnp.float32)


def with_spikes(drawn, own_key, source, target, blocks, factor):
    def block_of(position):
        return (jnp.arange(drawn.shape[position]) // (drawn.shape[position] // blocks)).reshape((-1,) + (1,) * (drawn.ndim - 1 - position))

    first = jax.random.permutation(own_key, blocks)[block_of(target)]
    far = (block_of(target) + blocks // 2) % blocks
    return jnp.where((block_of(source) == first) | (block_of(source) == far), factor * drawn, drawn)


def shard_levels(rng, extent, cuts, smallest, high):
    def one(axis_at, parts):
        heights = jax.random.uniform(jax.random.fold_in(jax.random.fold_in(rng, 6), axis_at), (parts,), jnp.float32, smallest / len(cuts), high / len(cuts))
        return jnp.repeat(jnp.exp(heights), extent[axis_at] // parts).reshape((-1,) + (1,) * (len(extent) - axis_at - 1))

    loudness = one(*cuts[0])
    for cut in cuts[1:]:
        loudness = loudness * one(*cut)
    return loudness


def bell_draw(rng, shape, spread, limit, cuts=(), held_as=jnp.bfloat16):
    loudness = shard_levels(rng, shape, cuts, -0.22, 0.18) if cuts else 1.0
    entries = jax.random.normal(rng, shape, jnp.float32) * spread * loudness
    return jnp.minimum(jnp.maximum(entries, -limit), limit).astype(held_as)


def gaussian_with(key, shape, deviation, reach, cuts, heavy, held_as=jnp.bfloat16):
    values = deviation * jax.random.normal(key, shape, jnp.float32)
    if cuts:
        values = values * shard_levels(key, shape, cuts, -0.22, 0.18)
    return jnp.clip(with_spikes(values, jax.random.fold_in(key, 3), *heavy), -reach, reach).astype(held_as)


def setup_inputs(seed: int = 0) -> dict:
    key_list = jax.random.split(jax.random.key(seed), 7)
    query_act = bell_draw(key_list[0], (TOKENS, D), 1.0, 6.0, ((0, 32), (1, 8)))
    key_act = bell_draw(key_list[1], (TOKENS, D), 1.0, 6.0, ((0, 32), (1, 8)))
    value_act = bell_draw(key_list[2], (TOKENS, D), 1.0, 6.0, ((0, 32), (1, 8)))
    filters = draw_filters(jax.random.fold_in(key_list[6], 71), 0)
    out_weight = bell_draw(key_list[4], (D, D), D ** -0.5, 0.09375, ((0, 32), (1, 8)))
    grad_out = gaussian_with(key_list[5], (TOKENS, D), 1.0, 6.0, ((0, 32), (1, 8)), (0, 1, 32, 2.75))
    return dict(query_act=query_act, key_act=key_act, value_act=value_act, filters=filters, out_weight=out_weight, grad_out=grad_out)


def reference(query_act, key_act, value_act, filters, out_weight, grad_out):
    length = query_act.shape[0]
    width = query_act.shape[1]
    taps = filters.shape[0]
    product = (key_act.astype(jnp.float32) * value_act.astype(jnp.float32)).astype(jnp.bfloat16)
    padded = jnp.concatenate([jnp.zeros((taps - 1, width), jnp.bfloat16), product], axis=0)

    def forward_tap(tap, total):
        window = lax.dynamic_slice_in_dim(padded, taps - 1 - tap, length, 0).astype(jnp.float32)
        return total + lax.dynamic_slice_in_dim(filters, tap, 1, 0) * window

    conv_out = lax.fori_loop(0, taps, forward_tap, jnp.zeros((length, width), jnp.float32))
    gated = (query_act.astype(jnp.float32) * conv_out).astype(jnp.bfloat16)
    grad_gated = jnp.dot(grad_out, out_weight, preferred_element_type=jnp.float32)
    out_blocks = grad_out.reshape(N_CTX, length // N_CTX, width)
    gated_blocks = gated.reshape(N_CTX, length // N_CTX, width)

    def add_block(total, pair):
        term = lax.dot_general(pair[0], pair[1], (((0,), (0,)), ((), ())), preferred_element_type=jnp.float32)
        return total + term, None

    weight_sum, unused = lax.scan(add_block, jnp.zeros((width, width), jnp.float32), (out_blocks, gated_blocks))
    grad_weight = weight_sum.astype(jnp.bfloat16)
    grad_query = (grad_gated * conv_out).astype(jnp.bfloat16)
    grad_acc = grad_gated * query_act.astype(jnp.float32)
    grad_padded = jnp.concatenate([grad_acc, jnp.zeros((taps - 1, width), jnp.float32)], axis=0)

    def adjoint_tap(tap, total):
        window = lax.dynamic_slice_in_dim(grad_padded, tap, length, 0)
        return total + lax.dynamic_slice_in_dim(filters, tap, 1, 0) * window

    grad_product = lax.fori_loop(0, taps, adjoint_tap, jnp.zeros((length, width), jnp.float32))
    grad_key = (grad_product * value_act.astype(jnp.float32)).astype(jnp.bfloat16)
    grad_value = (grad_product * key_act.astype(jnp.float32)).astype(jnp.bfloat16)

    def filter_tap(tap, result):
        window = lax.dynamic_slice_in_dim(padded, taps - 1 - tap, length, 0).astype(jnp.float32)
        row = jnp.sum(grad_acc * window, axis=0, keepdims=True)
        return lax.dynamic_update_slice_in_dim(result, row, tap, 0)

    grad_filters = lax.fori_loop(0, taps, filter_tap, jnp.zeros((taps, width), jnp.float32))
    return (grad_query, grad_key, grad_value, grad_filters, grad_weight)
```

```python
import jax
import jax.numpy as jnp
from jax import lax
from jax.experimental import pallas as pl
from jax.experimental.pallas import tpu as pltpu
from jax.sharding import PartitionSpec as P

MESH = pl.DeviceIdType.MESH
BF16 = jnp.bfloat16
F32 = jnp.float32


def lanes(group):
    return pl.ds(group * 128, 128)


def kernel(
    q_ref, k_ref, v_ref, f_ref, w_hbm, g_hbm,
    gq_ref, gk_ref, gv_ref, gf_ref, gw_ref,
    G, S, W, ext, conv, ga, gg, filt, gt_own, gt_sib,
    halo_s, halo_r, back_s, back_r,
    plus_s, plus_r, minus_s, minus_r, pair_s, pair_r, own_sum,
    taps, taps_sib, taps_mine, taps_parts, taps_all,
    send, recv, part_send, part_recv, all_send, all_recv, local_sem,
):
    ctx = lax.axis_index("ctx")
    t = lax.axis_index("tp")
    z = ctx // 4
    yh = lax.rem(ctx // 2, 2)
    core = lax.rem(ctx, 2)
    x = t // 2
    yl = lax.rem(t, 2)
    chip = ctx // 2

    def ctx_of(zz, hh, cc):
        return lax.rem(zz + 8, 8) * 4 + hh * 2 + cc

    def tp_of(xx, ll):
        return lax.rem(xx + 4, 4) * 2 + ll

    x_plus = (ctx, tp_of(x + 1, yl))
    x_minus = (ctx, tp_of(x - 1, yl))
    y_low = (ctx, tp_of(x, 1 - yl))
    z_plus = (ctx_of(z + 1, yh, core), t)
    z_minus = (ctx_of(z - 1, yh, core), t)
    y_high = (ctx_of(z, 1 - yh, core), t)
    sibling = (ctx_of(z, yh, 1 - core), t)
    after = (lax.rem(ctx + 1, 32), t)
    before = (lax.rem(ctx + 31, 32), t)
    beyond = (lax.rem(ctx + 31 + 2 * core, 32), t)

    def chip_device(other):
        return (other * 2 + core, t)

    started = []

    def push(src, dst, device):
        slot = len(started)
        copy = pltpu.make_async_remote_copy(
            src_ref=src, dst_ref=dst, send_sem=send.at[slot], recv_sem=recv.at[slot],
            device_id=device, device_id_type=MESH,
        )
        copy.start()
        started.append(copy)
        return copy

    own_copies = [pltpu.make_async_copy(w_hbm, W.at[ctx], local_sem.at[4])]
    for part in range(4):
        own_copies.append(
            pltpu.make_async_copy(
                g_hbm.at[:, lanes(part)], G.at[t, part // 2, part % 2], local_sem.at[part]
            )
        )
    for copy in own_copies:
        copy.start()

    barrier = pltpu.get_barrier_semaphore()
    for device in (x_plus, x_minus, y_low, sibling, beyond):
        pl.semaphore_signal(barrier, inc=1, device_id=device, device_id_type=MESH)

    def greet(step, carry):
        pl.semaphore_signal(
            barrier, inc=1, device_id=chip_device(lax.rem(chip + step, 16)), device_id_type=MESH
        )
        return carry

    lax.fori_loop(1, 16, greet, 0)

    for g in range(4):
        product = (k_ref[:, lanes(g)].astype(F32) * v_ref[:, lanes(g)].astype(F32)).astype(BF16)
        halo_s[:, lanes(g)] = product[384:]
        ext[g, 128:] = product.astype(F32)
        filt[g] = f_ref[:, lanes(g)]
    for copy in own_copies:
        copy.wait()
    pl.semaphore_wait(barrier, 20)

    halo = push(halo_s, halo_r, after)
    w_high = push(W.at[ctx], W.at[ctx], y_high)
    w_plus = {}
    w_minus = {}
    w_plus[1, 0] = push(W.at[ctx], W.at[ctx], z_plus)
    w_minus[1, 0] = push(W.at[ctx], W.at[ctx], z_minus)
    g_plus = push(G.at[t], G.at[t], x_plus)
    g_minus = push(G.at[t], G.at[t], x_minus)
    g_low = push(G.at[t], G.at[t], y_low)
    to_sib = []

    def share_w(slot):
        to_sib.append(push(W.at[slot], W.at[slot], sibling))

    def share_g(j):
        to_sib.append(push(G.at[j, :, 1 - core], S.at[j], sibling))

    share_w(ctx)
    share_g(t)

    def forward_w(step, b):
        hh = yh if b == 0 else 1 - yh
        if step == 0:
            w_high.wait_recv()
            slot = ctx_of(z, 1 - yh, core)
            w_plus[1, 1] = push(W.at[slot], W.at[slot], z_plus)
            w_minus[1, 1] = push(W.at[slot], W.at[slot], z_minus)
            share_w(slot)
            return
        w_plus[step, b].wait_recv()
        w_minus[step, b].wait_recv()
        low = ctx_of(z - step, hh, core)
        high = ctx_of(z + step, hh, core)
        if step < 3:
            w_plus[step + 1, b] = push(W.at[low], W.at[low], z_plus)
            w_minus[step + 1, b] = push(W.at[high], W.at[high], z_minus)
        elif step == 3:
            w_plus[4, b] = push(W.at[low, pl.ds(0, 64)], W.at[low, pl.ds(0, 64)], z_plus)
            w_minus[4, b] = push(W.at[high, pl.ds(64, 64)], W.at[high, pl.ds(64, 64)], z_minus)
        share_w(low)
        if step < 4:
            share_w(high)

    def forward_taps(b):
        def one(g, carry):
            def residue(r, acc):
                window = ext[g, pl.ds(b * 128 + 8 - r, 248), :]
                for k in range(16):
                    acc = acc + filt[g, pl.ds(8 * k + r, 1), :] * window[8 * (15 - k) : 8 * (15 - k) + 128]
                return acc

            conv[g, pl.ds(b * 128, 128), :] = lax.fori_loop(0, 8, residue, jnp.zeros((128, 128), F32))
            return carry

        lax.fori_loop(0, 4, one, 0)

    forward_taps(1)
    forward_w(0, 1)
    forward_w(1, 0)
    forward_taps(2)
    forward_w(1, 1)
    forward_taps(3)
    forward_w(2, 0)
    halo.wait_recv()
    for g in range(4):
        rim = halo_r[:, lanes(g)].astype(F32)
        ext[g, :128] = jnp.where(ctx == 0, 0.0, rim)
    forward_taps(0)
    forward_w(2, 1)

    b_minus, b_plus, b_far = tp_of(x - 1, yl), tp_of(x + 1, yl), tp_of(x + 2, yl)
    p_own, p_minus, p_plus, p_far = (
        tp_of(x, 1 - yl), tp_of(x - 1, 1 - yl), tp_of(x + 1, 1 - yl), tp_of(x + 2, 1 - yl)
    )

    def rows(j, start, size):
        return G.at[j, :, :, pl.ds(start, size)]

    def push_rows(j, start, size, device):
        return push(rows(j, start, size), rows(j, start, size), device)

    g_low.wait_recv()
    a_plus = push_rows(p_own, 112, 288, x_plus)
    a_minus = push_rows(p_own, 112, 288, x_minus)
    g_plus.wait_recv()
    half_plus = push_rows(b_minus, 0, 256, x_plus)
    low_rows = [push_rows(b_minus, 0, 112, y_low), push_rows(b_minus, 400, 112, y_low)]
    g_minus.wait_recv()
    half_minus = push_rows(b_plus, 256, 256, x_minus)
    low_rows += [push_rows(b_plus, 0, 112, y_low), push_rows(b_plus, 400, 112, y_low)]
    share_g(p_own)
    share_g(b_minus)
    share_g(b_plus)
    forward_w(3, 0)

    for g in range(4):
        gated = (q_ref[:, lanes(g)].astype(F32) * conv[g]).astype(BF16)
        gt_own[pl.ds(g * 128, 128), :] = gated.astype(F32).T.astype(BF16)
    gt_copy = push(gt_own, gt_sib, sibling)

    forward_w(3, 1)
    a_plus.wait_recv()
    far_plus = push_rows(p_minus, 112, 144, x_plus)
    a_minus.wait_recv()
    far_minus = push_rows(p_plus, 256, 144, x_minus)
    half_plus.wait_recv()
    low_rows.append(push_rows(b_far, 0, 112, y_low))
    half_minus.wait_recv()
    low_rows.append(push_rows(b_far, 400, 112, y_low))
    share_g(b_far)
    forward_w(4, 0)
    forward_w(4, 1)
    low_rows[0].wait_recv()
    low_rows[1].wait_recv()
    share_g(p_minus)
    low_rows[2].wait_recv()
    low_rows[3].wait_recv()
    share_g(p_plus)
    far_plus.wait_recv()
    far_minus.wait_recv()
    low_rows[4].wait_recv()
    low_rows[5].wait_recv()
    share_g(p_far)
    gt_copy.wait_recv()
    for copy in to_sib:
        copy.wait_recv()

    def term(j, h):
        mine = jnp.concatenate([G[j, yh, core], G[j, 1 - yh, core]], axis=1)
        theirs = jnp.concatenate([S[j, yh], S[j, 1 - yh]], axis=1)
        part = pl.ds(h * 256, 256)
        return jnp.dot(gt_own[part, :], mine, preferred_element_type=F32) + jnp.dot(
            gt_sib[part, :], theirs, preferred_element_type=F32
        )

    sent_plus = {}
    sent_minus = {}

    def send_plus(step, h):
        total = term(lax.rem(z + 5 - step, 8), h)
        if (step - 1, h) in sent_plus:
            sent_plus[step - 1, h].wait_recv()
            total = total + plus_r[step - 2, h].astype(F32)
        plus_s[step - 1, h] = total.astype(BF16)
        sent_plus[step, h] = push(plus_s.at[step - 1, h], plus_r.at[step - 1, h], z_plus)

    def send_minus(step, h):
        total = term(lax.rem(z + 3 + step, 8), h)
        if (step - 1, h) in sent_minus:
            sent_minus[step - 1, h].wait_recv()
            total = total + minus_r[step - 2, h].astype(F32)
        minus_s[step - 1, h] = total.astype(BF16)
        sent_minus[step, h] = push(minus_s.at[step - 1, h], minus_r.at[step - 1, h], z_minus)

    send_plus(1, 0)
    send_minus(1, 1)
    send_plus(2, 1)
    send_minus(2, 0)

    gg[...] = jnp.zeros((512, 512), F32)

    def gather_dot(j, carry):
        block = jnp.concatenate([G[j, 0, 0], G[j, 0, 1], G[j, 1, 0], G[j, 1, 1]], axis=1)
        gg[...] += jnp.dot(
            block, W[pl.ds(4 * j, 4)].reshape(512, 512), preferred_element_type=F32
        )
        return carry

    lax.fori_loop(0, 8, gather_dot, 0)
    for g in range(4):
        grad = gg[:, lanes(g)]
        gq_ref[:, lanes(g)] = (grad * conv[g]).astype(BF16)
        acc = grad * q_ref[:, lanes(g)].astype(F32)
        ga[g, :512] = acc
        back_s[:, lanes(g)] = acc[:128].astype(BF16)
    back = push(back_s, back_r, before)

    def filter_taps(g):
        def residue(r, carry):
            def block(b, sums):
                acc = ga[g, pl.ds(pl.multiple_of(b * 128, 128), 128), :].reshape(16, 8, 128)
                window = ext[g, pl.ds(b * 128 + 8 - r, 248), :].reshape(31, 8, 128)
                return tuple(
                    sums[k] + jnp.sum(acc * window[15 - k : 31 - k], axis=0) for k in range(16)
                )

            sums = lax.fori_loop(0, 4, block, tuple(jnp.zeros((8, 128), F32) for _ in range(16)))
            for k in range(16):
                taps[g, pl.ds(8 * k + r, 1), :] = jnp.sum(sums[k], axis=0, keepdims=True)
            return carry

        lax.fori_loop(0, 8, residue, 0)

    def adjoint_taps(g):
        def block(b, carry):
            here = pl.ds(pl.multiple_of(b * 128, 128), 128)

            def residue(r, acc):
                window = ga[g, pl.ds(b * 128 + r, 248), :]
                for k in range(16):
                    acc = acc + filt[g, pl.ds(8 * k + r, 1), :] * window[8 * k : 8 * k + 128]
                return acc

            grad = lax.fori_loop(0, 8, residue, jnp.zeros((128, 128), F32))
            gk_ref[here, lanes(g)] = (grad * v_ref[here, lanes(g)].astype(F32)).astype(BF16)
            gv_ref[here, lanes(g)] = (grad * k_ref[here, lanes(g)].astype(F32)).astype(BF16)
            return carry

        lax.fori_loop(0, 4, block, 0)

    send_plus(2, 0)
    send_minus(2, 1)
    filter_taps(0)
    send_plus(3, 1)
    send_minus(3, 0)
    filter_taps(1)
    send_plus(3, 0)
    send_minus(3, 1)
    filter_taps(2)
    send_plus(4, 1)
    send_minus(4, 0)
    filter_taps(3)
    half = pl.ds(2 * core, 2)
    other_half = pl.ds(2 - 2 * core, 2)
    tap_pair = push(taps.at[other_half], taps_sib, sibling)
    send_plus(4, 0)
    send_minus(4, 1)

    back.wait_recv()
    for g in range(4):
        rim = back_r[:, lanes(g)].astype(F32)
        ga[g, 512:] = jnp.where(ctx == 31, 0.0, rim)
    adjoint_taps(0)

    tap_pair.wait_recv()
    taps_mine[...] = taps[half] + taps_sib[...]

    def piece(ref, owner):
        return ref.at[:, pl.ds(pl.multiple_of(owner * 8, 8), 8), :]

    def part_copy(step):
        owner = lax.rem(chip + step, 16)
        return pltpu.make_async_remote_copy(
            src_ref=piece(taps_mine, owner), dst_ref=taps_parts.at[step],
            send_sem=part_send.at[step], recv_sem=part_recv.at[step],
            device_id=chip_device(owner), device_id_type=MESH,
        )

    def all_copy(step):
        return pltpu.make_async_remote_copy(
            src_ref=taps_parts.at[0], dst_ref=piece(taps_all.at[half], chip),
            send_sem=all_send.at[step], recv_sem=all_recv.at[step],
            device_id=chip_device(lax.rem(chip + step, 16)), device_id_type=MESH,
        )

    def loop(action):
        def body(step, carry):
            action(step)
            return carry

        lax.fori_loop(1, 16, body, 0)

    loop(lambda step: part_copy(step).start())
    adjoint_taps(1)
    loop(lambda step: part_copy(step).wait_recv())
    mine = pl.ds(pl.multiple_of(chip * 8, 8), 8)
    total = taps_mine[:, mine, :]
    for step in range(1, 16):
        total = total + taps_parts[step]
    taps_parts[0] = total
    taps_all[half, mine, :] = total
    loop(lambda step: all_copy(step).start())

    for h in range(2):
        total = term(z, h)
        sent_plus[4, h].wait_recv()
        sent_minus[4, h].wait_recv()
        total = total + plus_r[3, h].astype(F32) + minus_r[3, h].astype(F32)
        own_sum[pl.ds(h * 256, 256), :] = total[:, :128]
        pair_s[pl.ds(h * 256, 256), :] = total[:, 128:].astype(BF16)
    pair = push(pair_s, pair_r, y_high)
    adjoint_taps(2)
    loop(lambda step: all_copy(step).wait_recv())
    spread = push(taps_all.at[half], taps_all.at[half], sibling)
    adjoint_taps(3)
    pair.wait_recv()
    gw_ref[...] = (own_sum[...] + pair_r[...].astype(F32)).T.astype(BF16)
    spread.wait_recv()
    for g in range(4):
        gf_ref[:, lanes(g)] = taps_all[g]
    for copy in started:
        copy.wait_send()
    loop(lambda step: part_copy(step).wait_send())
    loop(lambda step: all_copy(step).wait_send())


def local(query_act, key_act, value_act, filters, out_weight, grad_out):
    vmem = pl.BlockSpec(memory_space=pltpu.VMEM)
    hbm = pl.BlockSpec(memory_space=pl.ANY)
    shape = jax.ShapeDtypeStruct
    tokens = shape((512, 512), BF16)
    return pl.pallas_call(
        kernel,
        out_shape=(tokens, tokens, tokens, shape((128, 512), F32), shape((128, 512), BF16)),
        in_specs=[vmem, vmem, vmem, vmem, hbm, hbm],
        out_specs=(vmem,) * 5,
        scratch_shapes=[
            pltpu.VMEM((8, 2, 2, 512, 128), BF16),
            pltpu.VMEM((8, 2, 512, 128), BF16),
            pltpu.VMEM((32, 128, 512), BF16),
            pltpu.VMEM((4, 640, 128), F32),
            pltpu.VMEM((4, 512, 128), F32),
            pltpu.VMEM((4, 640, 128), F32),
            pltpu.VMEM((512, 512), F32),
            pltpu.VMEM((4, 128, 128), F32),
            pltpu.VMEM((512, 512), BF16),
            pltpu.VMEM((512, 512), BF16),
            pltpu.VMEM((128, 512), BF16),
            pltpu.VMEM((128, 512), BF16),
            pltpu.VMEM((128, 512), BF16),
            pltpu.VMEM((128, 512), BF16),
            pltpu.VMEM((4, 2, 256, 256), BF16),
            pltpu.VMEM((4, 2, 256, 256), BF16),
            pltpu.VMEM((4, 2, 256, 256), BF16),
            pltpu.VMEM((4, 2, 256, 256), BF16),
            pltpu.VMEM((512, 128), BF16),
            pltpu.VMEM((512, 128), BF16),
            pltpu.VMEM((512, 128), F32),
            pltpu.VMEM((4, 128, 128), F32),
            pltpu.VMEM((2, 128, 128), F32),
            pltpu.VMEM((2, 128, 128), F32),
            pltpu.VMEM((16, 2, 8, 128), F32),
            pltpu.VMEM((4, 128, 128), F32),
            pltpu.SemaphoreType.DMA((80,)),
            pltpu.SemaphoreType.DMA((80,)),
            pltpu.SemaphoreType.DMA((16,)),
            pltpu.SemaphoreType.DMA((16,)),
            pltpu.SemaphoreType.DMA((16,)),
            pltpu.SemaphoreType.DMA((16,)),
            pltpu.SemaphoreType.DMA((5,)),
        ],
        compiler_params=pltpu.CompilerParams(
            collective_id=0, has_side_effects=True, vmem_limit_bytes=52 * 2**20
        ),
        cost_estimate=pl.CostEstimate(flops=2 * 10**9 * 2, bytes_accessed=5 * 2**20, transcendentals=0),
        name="block_grads",
    )(query_act, key_act, value_act, filters, out_weight, grad_out)


def solution(mesh):
    placed = (
        P("ctx", "tp"),
        P("ctx", "tp"),
        P("ctx", "tp"),
        P(None, "tp"),
        P("ctx", "tp"),
        P("ctx", "tp"),
    )
    return jax.shard_map(
        local,
        mesh=mesh,
        in_specs=placed,
        out_specs=(P("ctx", "tp"), P("ctx", "tp"), P("ctx", "tp"), P(None, "tp"), P("ctx", "tp")),
        check_vma=False,
    )
```

```python
import jax
import jax.numpy as jnp
from jax import lax
from jax.experimental import pallas as pl
from jax.experimental.pallas import tpu as pltpu
from jax.sharding import PartitionSpec as P

MESH = pl.DeviceIdType.MESH
BF16 = jnp.bfloat16
F32 = jnp.float32


def lanes(group):
    return pl.ds(group * 128, 128)


LEVELS = 2
LEAF = 16 >> LEVELS
SUMS = 3**LEVELS * LEAF


def split_taps(taps, levels):
    if levels == 0:
        return list(taps)
    even, odd = taps[0::2], taps[1::2]
    both = [a + b for a, b in zip(even, odd)]
    return (
        split_taps(both, levels - 1) + split_taps(even, levels - 1) + split_taps(odd, levels - 1)
    )


def split_rows(rows, levels):
    if levels == 0:
        return [rows]
    even, odd = rows[0::2], rows[1::2]
    here = [a - b for a, b in zip(even[:-1], odd)]
    moved = [a - b for a, b in zip(even[1:], odd)]
    return (
        split_rows(odd, levels - 1) + split_rows(here, levels - 1) + split_rows(moved, levels - 1)
    )


def join_sums(sums, levels):
    if levels == 0:
        return list(sums)
    third = len(sums) // 3
    both, even, odd = (
        join_sums(sums[i * third : (i + 1) * third], levels - 1) for i in range(3)
    )
    joined = []
    for p, a, b in zip(both, even, odd):
        joined += [p + a, p + b]
    return joined


def add_taps(sums, window, tap):
    vectors = [window[8 * i : 8 * i + 8] for i in range(31)]
    result = []
    for leaf, rows in enumerate(split_rows(vectors, LEVELS)):
        taps = [tap(leaf * LEAF + k) for k in range(LEAF)]
        for m in range(LEAF):
            total = sums[leaf * LEAF + m]
            for k in range(LEAF):
                total = total + taps[k] * rows[m + k]
            result.append(total)
    return tuple(result)


def no_sums():
    return tuple(jnp.zeros((8, 128), F32) for _ in range(SUMS))


def kernel(
    q_hbm, k_hbm, v_hbm, f_hbm, w_hbm, g_hbm,
    gq_hbm, gk_hbm, gv_hbm, gf_hbm, gw_hbm,
    q_ref, k_ref, v_ref, gq_ref, gk_ref, gv_ref, gw_ref,
    G, S, W, ext, conv, ga, gg, filt, filt_ahead, filt_back, cotangent, gt_own, gt_sib,
    halo_s, halo_r, back_s, back_r,
    part, plus_s, plus_r, minus_s, minus_r, pair_s, pair_r,
    taps, taps_sib, taps_mine, taps_parts, taps_all,
    send, recv, part_send, part_recv, all_send, all_recv, in_sem, out_sem,
):
    ctx = lax.axis_index("ctx")
    t = lax.axis_index("tp")
    z = ctx // 4
    yh = lax.rem(ctx // 2, 2)
    core = lax.rem(ctx, 2)
    x = t // 2
    yl = lax.rem(t, 2)
    chip = ctx // 2

    def ctx_of(zz, hh, cc):
        return lax.rem(zz + 8, 8) * 4 + hh * 2 + cc

    def tp_of(xx, ll):
        return lax.rem(xx + 4, 4) * 2 + ll

    x_plus = (ctx, tp_of(x + 1, yl))
    x_minus = (ctx, tp_of(x - 1, yl))
    y_low = (ctx, tp_of(x, 1 - yl))
    z_plus = (ctx_of(z + 1, yh, core), t)
    z_minus = (ctx_of(z - 1, yh, core), t)
    y_high = (ctx_of(z, 1 - yh, core), t)
    sibling = (ctx_of(z, yh, 1 - core), t)
    after = (lax.rem(ctx + 1, 32), t)
    before = (lax.rem(ctx + 31, 32), t)
    beyond = (lax.rem(ctx + 31 + 2 * core, 32), t)

    def chip_device(other):
        return (other * 2 + core, t)

    started = []

    def push(src, dst, device):
        slot = len(started)
        copy = pltpu.make_async_remote_copy(
            src_ref=src, dst_ref=dst, send_sem=send.at[slot], recv_sem=recv.at[slot],
            device_id=device, device_id_type=MESH,
        )
        copy.start()
        started.append(copy)
        return copy

    barrier = pltpu.get_barrier_semaphore()
    for device in (x_plus, x_minus, y_low, sibling, beyond):
        pl.semaphore_signal(barrier, inc=1, device_id=device, device_id_type=MESH)

    def greet(step, carry):
        pl.semaphore_signal(
            barrier, inc=1, device_id=chip_device(lax.rem(chip + step, 16)), device_id_type=MESH
        )
        return carry

    lax.fori_loop(1, 16, greet, 0)

    loads = []

    def load(src, dst):
        copy = pltpu.make_async_copy(src, dst, in_sem.at[len(loads)])
        copy.start()
        loads.append(copy)

    for g in range(4):
        load(g_hbm.at[:, lanes(g)], G.at[t, g // 2, g % 2])
    load(w_hbm, W.at[ctx])
    load(k_hbm, k_ref)
    load(v_hbm, v_ref)
    for g in range(4):
        load(f_hbm.at[:, lanes(g)], filt.at[g])
    load(q_hbm, q_ref)

    stores = []

    def store(src, dst):
        copy = pltpu.make_async_copy(src, dst, out_sem.at[len(stores)])
        copy.start()
        stores.append(copy)

    for copy in loads[:5]:
        copy.wait()
    pl.semaphore_wait(barrier, 20)

    pieces = ((1 - yh, 256, 256, 48), (yh, 256, 256, 48), (1 - yh, 0, 256, 48), (yh, 0, 256, 48))
    b_minus, b_plus, b_far = tp_of(x - 1, yl), tp_of(x + 1, yl), tp_of(x + 2, yl)
    p_own, p_minus, p_plus, p_far = (
        tp_of(x, 1 - yl), tp_of(x - 1, 1 - yl), tp_of(x + 1, 1 - yl), tp_of(x + 2, 1 - yl)
    )
    flight = {}
    shared = {}

    def push_rows(p, j, start, size, device):
        hs, first = pieces[p][:2]
        ref = G.at[j, hs, :, pl.ds(first + start, size)]
        return push(ref, ref, device)

    def share_g(p, j):
        hs, first, count, edge = pieces[p]
        here = pl.ds(first, count)
        shared.setdefault(p, []).append(
            push(G.at[j, hs, 1 - core, here], S.at[j, hs, here], sibling)
        )

    def gather_0(p):
        count = pieces[p][2]
        flight[p, "plus"] = push_rows(p, t, 0, count, x_plus)
        flight[p, "minus"] = push_rows(p, t, 0, count, x_minus)
        flight[p, "low"] = push_rows(p, t, 0, count, y_low)
        share_g(p, t)

    def gather_1(p):
        hs, first, count, edge = pieces[p]
        half = count // 2
        flight[p, "low"].wait_recv()
        flight[p, "a_plus"] = push_rows(p, p_own, edge, count - 2 * edge, x_plus)
        flight[p, "a_minus"] = push_rows(p, p_own, edge, count - 2 * edge, x_minus)
        flight[p, "plus"].wait_recv()
        flight[p, "half_plus"] = push_rows(p, b_minus, 0, half, x_plus)
        flight[p, "low_0"] = push_rows(p, b_minus, 0, edge, y_low)
        flight[p, "low_1"] = push_rows(p, b_minus, count - edge, edge, y_low)
        flight[p, "minus"].wait_recv()
        flight[p, "half_minus"] = push_rows(p, b_plus, half, half, x_minus)
        flight[p, "low_2"] = push_rows(p, b_plus, 0, edge, y_low)
        flight[p, "low_3"] = push_rows(p, b_plus, count - edge, edge, y_low)
        share_g(p, p_own)
        share_g(p, b_minus)
        share_g(p, b_plus)

    def gather_2(p):
        hs, first, count, edge = pieces[p]
        half = count // 2
        flight[p, "a_plus"].wait_recv()
        flight[p, "far_plus"] = push_rows(p, p_minus, edge, half - edge, x_plus)
        flight[p, "a_minus"].wait_recv()
        flight[p, "far_minus"] = push_rows(p, p_plus, half, half - edge, x_minus)
        flight[p, "half_plus"].wait_recv()
        flight[p, "low_4"] = push_rows(p, b_far, 0, edge, y_low)
        flight[p, "half_minus"].wait_recv()
        flight[p, "low_5"] = push_rows(p, b_far, count - edge, edge, y_low)
        share_g(p, b_far)

    def gather_3(p):
        for name in ("low_0", "low_1"):
            flight[p, name].wait_recv()
        share_g(p, p_minus)
        for name in ("low_2", "low_3"):
            flight[p, name].wait_recv()
        share_g(p, p_plus)
        for name in ("far_plus", "far_minus", "low_4", "low_5"):
            flight[p, name].wait_recv()
        share_g(p, p_far)

    w_plus = {}
    w_minus = {}
    w_shared = []

    def share_w(slot):
        w_shared.append(push(W.at[slot], W.at[slot], sibling))

    def forward_w(step, b):
        hh = yh if b == 0 else 1 - yh
        if step == 0:
            w_high.wait_recv()
            slot = ctx_of(z, 1 - yh, core)
            w_plus[1, 1] = push(W.at[slot], W.at[slot], z_plus)
            w_minus[1, 1] = push(W.at[slot], W.at[slot], z_minus)
            share_w(slot)
            return
        w_plus[step, b].wait_recv()
        w_minus[step, b].wait_recv()
        low = ctx_of(z - step, hh, core)
        high = ctx_of(z + step, hh, core)
        if step < 3:
            w_plus[step + 1, b] = push(W.at[low], W.at[low], z_plus)
            w_minus[step + 1, b] = push(W.at[high], W.at[high], z_minus)
        elif step == 3:
            w_plus[4, b] = push(W.at[low, pl.ds(0, 64)], W.at[low, pl.ds(0, 64)], z_plus)
            w_minus[4, b] = push(W.at[high, pl.ds(64, 64)], W.at[high, pl.ds(64, 64)], z_minus)
        share_w(low)
        if step < 4:
            share_w(high)

    def split_filters():
        for g in range(4):
            by_8 = [filt[g, 8 * k : 8 * k + 8, :] for k in range(16)]
            for i, row in enumerate(split_taps(by_8[::-1], LEVELS)):
                filt_back[g, 8 * i : 8 * i + 8, :] = row
            for i, row in enumerate(split_taps(by_8, LEVELS)):
                filt_ahead[g, 8 * i : 8 * i + 8, :] = row

    def forward_taps(b, group, count):
        def one(g, carry):
            def residue(r, sums):
                return add_taps(
                    sums, ext[g, pl.ds(b * 128 + 8 - r, 248), :],
                    lambda i: jnp.broadcast_to(filt_back[g, pl.ds(8 * i + r, 1), :], (8, 128)),
                )

            for m, row in enumerate(join_sums(lax.fori_loop(0, 8, residue, no_sums()), LEVELS)):
                conv[g, pl.ds(b * 128 + 8 * m, 8), :] = row
            return carry

        lax.fori_loop(group, group + count, one, 0)

    def filter_taps(g, first_block):
        for n in range(2):
            start = (first_block + n) * 128
            by_8 = [ga[g, start + 8 * k : start + 8 * k + 8, :] for k in range(16)]
            for i, row in enumerate(split_taps(by_8, LEVELS)):
                cotangent[n, 8 * i : 8 * i + 8, :] = row

        def residue(r, carry):
            def block(n, sums):
                return add_taps(
                    sums, ext[g, pl.ds((first_block + n) * 128 + 8 - r, 248), :],
                    lambda i: cotangent[n, 8 * i : 8 * i + 8, :],
                )

            sums = join_sums(lax.fori_loop(0, 2, block, no_sums()), LEVELS)
            for k in range(16):
                row = jnp.sum(sums[15 - k], axis=0, keepdims=True)
                if first_block == 0:
                    row += taps[g, pl.ds(8 * k + r, 1), :]
                taps[g, pl.ds(8 * k + r, 1), :] = row
            return carry

        lax.fori_loop(0, 8, residue, 0)

    def adjoint_taps(b):
        def one(g, carry):
            def residue(r, sums):
                return add_taps(
                    sums, ga[g, pl.ds(b * 128 + r, 248), :],
                    lambda i: jnp.broadcast_to(filt_ahead[g, pl.ds(8 * i + r, 1), :], (8, 128)),
                )

            sums = join_sums(lax.fori_loop(0, 8, residue, no_sums()), LEVELS)
            side = pl.ds(pl.multiple_of(g * 128, 128), 128)
            for m in range(0, 16, 2):
                here = pl.ds(b * 128 + 8 * m, 16)
                grad = jnp.concatenate([sums[m], sums[m + 1]], axis=0)
                gk_ref[here, side] = (grad * v_ref[here, side].astype(F32)).astype(BF16)
                gv_ref[here, side] = (grad * k_ref[here, side].astype(F32)).astype(BF16)
            return carry

        lax.fori_loop(0, 4, one, 0)

    def terms(r, s):
        hs = 1 - yh if r == 0 else yh
        ahead = lax.rem(z + 4 - s, 8)
        behind = lax.rem(z + 4 + s, 8) if s else z
        mine = jnp.concatenate([G[ahead, hs, core], G[behind, hs, core]], axis=1)
        theirs = jnp.concatenate([S[ahead, hs], S[behind, hs]], axis=1)
        part[r, s] = jnp.dot(gt_own[...], mine, preferred_element_type=F32) + jnp.dot(
            gt_sib[...], theirs, preferred_element_type=F32
        )

    sent_plus = {}
    sent_minus = {}

    def send_plus(r, step, h):
        total = part[r, step - 1, pl.ds(256 * h, 256), :128]
        if (r, step - 1, h) in sent_plus:
            sent_plus[r, step - 1, h].wait_recv()
            total = total + plus_r[r, step - 2, h].astype(F32)
        plus_s[r, step - 1, h] = total.astype(BF16)
        sent_plus[r, step, h] = push(plus_s.at[r, step - 1, h], plus_r.at[r, step - 1, h], z_plus)

    def send_minus(r, step, h):
        columns = pl.ds(0 if step == 1 else 128, 128)
        total = part[r, step - 1, pl.ds(256 * h, 256), columns]
        if (r, step - 1, h) in sent_minus:
            sent_minus[r, step - 1, h].wait_recv()
            total = total + minus_r[r, step - 2, h].astype(F32)
        minus_s[r, step - 1, h] = total.astype(BF16)
        sent_minus[r, step, h] = push(
            minus_s.at[r, step - 1, h], minus_r.at[r, step - 1, h], z_minus
        )

    def reduce_start(r):
        terms(r, 0)
        send_plus(r, 1, 0)
        send_minus(r, 1, 1)
        terms(r, 1)
        send_plus(r, 2, 1)
        send_minus(r, 2, 0)
        terms(r, 2)
        terms(r, 3)

    def reduce_step(r, n):
        step, late = ((2, 1), (3, 0), (3, 1), (4, 0), (4, 1))[n]
        send_plus(r, step, 1 - late)
        send_minus(r, step, late)

    def reduced(r, h):
        sent_plus[r, 4, h].wait_recv()
        sent_minus[r, 4, h].wait_recv()
        return (
            part[r, 0, pl.ds(256 * h, 256), 128:]
            + plus_r[r, 3, h].astype(F32)
            + minus_r[r, 3, h].astype(F32)
        )

    def accumulate(first, count):
        here = pl.ds(first, count)
        for n in range(4):
            block = jnp.concatenate(
                [G[2 * n + i // 4, (i // 2) % 2, i % 2, here] for i in range(8)], axis=1
            )
            grad = jnp.dot(block, W[pl.ds(8 * n, 8)].reshape(1024, 512), preferred_element_type=F32)
            gg[here, :] = grad if n == 0 else gg[here, :] + grad

    def finish_rows(first, count):
        here = pl.ds(first, count)
        for g in range(4):
            grad = gg[here, lanes(g)]
            gq_ref[here, lanes(g)] = (grad * conv[g, here, :]).astype(BF16)
            ga[g, here, :] = grad * q_ref[here, lanes(g)].astype(F32)

    def gate(groups):
        for g in groups:
            gated = (q_ref[:, lanes(g)].astype(F32) * conv[g]).astype(BF16)
            gt_own[pl.ds(g * 128, 128), :] = gated.astype(F32).T.astype(BF16)

    half = pl.ds(2 * core, 2)
    other_half = pl.ds(2 - 2 * core, 2)

    def piece(ref, owner):
        return ref.at[:, pl.ds(pl.multiple_of(owner * 8, 8), 8), :]

    def part_copy(step):
        owner = lax.rem(chip + step, 16)
        return pltpu.make_async_remote_copy(
            src_ref=piece(taps_mine, owner), dst_ref=taps_parts.at[step],
            send_sem=part_send.at[step], recv_sem=part_recv.at[step],
            device_id=chip_device(owner), device_id_type=MESH,
        )

    def all_copy(step):
        return pltpu.make_async_remote_copy(
            src_ref=taps_parts.at[0], dst_ref=piece(taps_all.at[half], chip),
            send_sem=all_send.at[step], recv_sem=all_recv.at[step],
            device_id=chip_device(lax.rem(chip + step, 16)), device_id_type=MESH,
        )

    def loop(action):
        def body(step, carry):
            action(step)
            return carry

        lax.fori_loop(1, 16, body, 0)

    gather_0(0)
    w_high = push(W.at[ctx], W.at[ctx], y_high)
    w_plus[1, 0] = push(W.at[ctx], W.at[ctx], z_plus)
    w_minus[1, 0] = push(W.at[ctx], W.at[ctx], z_minus)
    share_w(ctx)
    for copy in loads[5:]:
        copy.wait()
    split_filters()
    for g in range(4):
        product = (k_ref[:, lanes(g)].astype(F32) * v_ref[:, lanes(g)].astype(F32)).astype(BF16)
        halo_s[:, lanes(g)] = product[384:]
        ext[g, 128:] = product.astype(F32)
    halo = push(halo_s, halo_r, after)
    gather_0(1)
    forward_taps(1, 0, 4)
    forward_w(0, 1)
    gather_1(0)
    gather_0(2)
    forward_w(1, 0)
    forward_taps(2, 0, 4)
    gather_1(1)
    forward_taps(3, 0, 3)
    forward_w(1, 1)
    gather_2(0)
    gather_0(3)
    forward_taps(3, 3, 1)
    forward_w(2, 0)
    halo.wait_recv()
    for g in range(4):
        rim = halo_r[:, lanes(g)].astype(F32)
        ext[g, :128] = jnp.where(ctx == 0, 0.0, rim)
    gather_1(2)
    forward_taps(0, 0, 4)
    forward_w(2, 1)
    gate((0,))
    gather_2(1)
    gate((1,))
    forward_w(3, 0)
    gate((2,))
    gather_1(3)
    gate((3,))
    gt_copy = push(gt_own, gt_sib, sibling)
    gather_3(0)
    forward_w(3, 1)
    forward_w(4, 0)
    gather_2(2)
    forward_w(4, 1)
    gather_3(1)
    for copy in w_shared:
        copy.wait_recv()
    accumulate(256, 256)
    finish_rows(256, 256)
    gather_2(3)
    filter_taps(0, 2)
    filter_taps(1, 2)
    gather_3(2)
    gt_copy.wait_recv()
    for p in (0, 2):
        for copy in shared[p]:
            copy.wait_recv()
    reduce_start(0)
    filter_taps(2, 2)
    gather_3(3)
    for p in (1, 3):
        for copy in shared[p]:
            copy.wait_recv()
    reduce_start(1)
    accumulate(0, 256)
    finish_rows(0, 256)
    store(gq_ref, gq_hbm)
    for g in range(4):
        back_s[:, lanes(g)] = ga[g, :128, :].astype(BF16)
    back = push(back_s, back_r, before)
    reduce_step(0, 0)
    filter_taps(3, 2)
    filter_taps(0, 0)
    reduce_step(1, 0)
    filter_taps(1, 0)
    reduce_step(0, 1)
    filter_taps(2, 0)
    reduce_step(1, 1)
    filter_taps(3, 0)
    tap_pair = push(taps.at[other_half], taps_sib, sibling)
    reduce_step(0, 2)
    adjoint_taps(2)
    tap_pair.wait_recv()
    taps_mine[...] = taps[half] + taps_sib[...]
    loop(lambda step: part_copy(step).start())
    reduce_step(1, 2)
    adjoint_taps(1)
    reduce_step(0, 3)
    loop(lambda step: part_copy(step).wait_recv())
    mine = pl.ds(pl.multiple_of(chip * 8, 8), 8)
    total = taps_mine[:, mine, :]
    for step in range(1, 16):
        total = total + taps_parts[step]
    taps_parts[0] = total
    taps_all[half, mine, :] = total
    loop(lambda step: all_copy(step).start())
    reduce_step(1, 3)
    adjoint_taps(0)
    reduce_step(0, 4)
    reduce_step(1, 4)
    back.wait_recv()
    for g in range(4):
        rim = back_r[:, lanes(g)].astype(F32)
        ga[g, 512:] = jnp.where(ctx == 31, 0.0, rim)
    loop(lambda step: all_copy(step).wait_recv())
    spread = push(taps_all.at[half], taps_all.at[half], sibling)
    for h in range(2):
        pair_s[pl.ds(256 * h, 256), :] = reduced(0, h).astype(BF16)
    pair = push(pair_s, pair_r, y_high)
    adjoint_taps(3)
    store(gk_ref, gk_hbm)
    store(gv_ref, gv_hbm)
    spread.wait_recv()
    for g in range(4):
        store(taps_all.at[g], gf_hbm.at[:, lanes(g)])
    totals = [reduced(1, h) for h in range(2)]
    pair.wait_recv()
    for h in range(2):
        rows = pl.ds(256 * h, 256)
        gw_ref[:, rows] = (totals[h] + pair_r[rows, :].astype(F32)).T.astype(BF16)
    store(gw_ref, gw_hbm)
    for copy in started:
        copy.wait_send()
    loop(lambda step: part_copy(step).wait_send())
    loop(lambda step: all_copy(step).wait_send())
    for copy in stores:
        copy.wait()


def local(query_act, key_act, value_act, filters, out_weight, grad_out):
    hbm = pl.BlockSpec(memory_space=pl.ANY)
    shape = jax.ShapeDtypeStruct
    tokens = shape((512, 512), BF16)
    block = pltpu.VMEM((512, 512), BF16)
    rim = pltpu.VMEM((128, 512), BF16)
    sums = pltpu.VMEM((2, 4, 2, 256, 128), BF16)
    return pl.pallas_call(
        kernel,
        out_shape=(tokens, tokens, tokens, shape((128, 512), F32), shape((128, 512), BF16)),
        in_specs=[hbm] * 6,
        out_specs=(hbm,) * 5,
        scratch_shapes=[
            block, block, block, block, block, block, rim,
            pltpu.VMEM((8, 2, 2, 512, 128), BF16),
            pltpu.VMEM((8, 2, 512, 128), BF16),
            pltpu.VMEM((32, 128, 512), BF16),
            pltpu.VMEM((4, 640, 128), F32),
            pltpu.VMEM((4, 512, 128), F32),
            pltpu.VMEM((4, 640, 128), F32),
            pltpu.VMEM((512, 512), F32),
            pltpu.VMEM((4, 128, 128), F32),
            pltpu.VMEM((4, 8 * SUMS, 128), F32),
            pltpu.VMEM((4, 8 * SUMS, 128), F32),
            pltpu.VMEM((2, 8 * SUMS, 128), F32),
            block, block,
            rim, rim, rim, rim,
            pltpu.VMEM((2, 4, 512, 256), F32),
            sums, sums, sums, sums,
            pltpu.VMEM((512, 128), BF16),
            pltpu.VMEM((512, 128), BF16),
            pltpu.VMEM((4, 128, 128), F32),
            pltpu.VMEM((2, 128, 128), F32),
            pltpu.VMEM((2, 128, 128), F32),
            pltpu.VMEM((16, 2, 8, 128), F32),
            pltpu.VMEM((4, 128, 128), F32),
            pltpu.SemaphoreType.DMA((170,)),
            pltpu.SemaphoreType.DMA((170,)),
            pltpu.SemaphoreType.DMA((16,)),
            pltpu.SemaphoreType.DMA((16,)),
            pltpu.SemaphoreType.DMA((16,)),
            pltpu.SemaphoreType.DMA((16,)),
            pltpu.SemaphoreType.DMA((12,)),
            pltpu.SemaphoreType.DMA((8,)),
        ],
        compiler_params=pltpu.CompilerParams(
            collective_id=0, has_side_effects=True, vmem_limit_bytes=60 * 2**20
        ),
        cost_estimate=pl.CostEstimate(flops=4 * 10**9, bytes_accessed=5 * 2**20, transcendentals=0),
        name="block_grads",
    )(query_act, key_act, value_act, filters, out_weight, grad_out)


def solution(mesh):
    placed = (
        P("ctx", "tp"),
        P("ctx", "tp"),
        P("ctx", "tp"),
        P(None, "tp"),
        P("ctx", "tp"),
        P("ctx", "tp"),
    )
    return jax.shard_map(
        local,
        mesh=mesh,
        in_specs=placed,
        out_specs=(P("ctx", "tp"), P("ctx", "tp"), P("ctx", "tp"), P(None, "tp"), P("ctx", "tp")),
        check_vma=False,
    )
```

```python
import jax
import jax.numpy as jnp
from jax import lax
from jax.experimental import pallas as pl
from jax.experimental.pallas import tpu as pltpu
from jax.sharding import PartitionSpec as P

MESH = pl.DeviceIdType.MESH
BF16 = jnp.bfloat16
F32 = jnp.float32


def lanes(group):
    return pl.ds(group * 128, 128)


LEVELS = 2
LEAF = 16 >> LEVELS
SUMS = 3**LEVELS * LEAF


def split_taps(taps, levels):
    if levels == 0:
        return list(taps)
    even, odd = taps[0::2], taps[1::2]
    both = [a + b for a, b in zip(even, odd)]
    return (
        split_taps(both, levels - 1) + split_taps(even, levels - 1) + split_taps(odd, levels - 1)
    )


def split_rows(rows, levels):
    if levels == 0:
        return [rows]
    even, odd = rows[0::2], rows[1::2]
    here = [a - b for a, b in zip(even[:-1], odd)]
    moved = [a - b for a, b in zip(even[1:], odd)]
    return (
        split_rows(odd, levels - 1) + split_rows(here, levels - 1) + split_rows(moved, levels - 1)
    )


def join_sums(sums, levels):
    if levels == 0:
        return list(sums)
    third = len(sums) // 3
    both, even, odd = (
        join_sums(sums[i * third : (i + 1) * third], levels - 1) for i in range(3)
    )
    joined = []
    for p, a, b in zip(both, even, odd):
        joined += [p + a, p + b]
    return joined


def add_taps(sums, window, tap):
    vectors = [window[8 * i : 8 * i + 8] for i in range(31)]
    result = []
    for leaf, rows in enumerate(split_rows(vectors, LEVELS)):
        taps = [tap(leaf * LEAF + k) for k in range(LEAF)]
        for m in range(LEAF):
            total = sums[leaf * LEAF + m]
            for k in range(LEAF):
                total = total + taps[k] * rows[m + k]
            result.append(total)
    return tuple(result)


def no_sums():
    return tuple(jnp.zeros((8, 128), F32) for _ in range(SUMS))


def kernel(
    q_hbm, k_hbm, v_hbm, f_hbm, w_hbm, g_hbm,
    gq_hbm, gk_hbm, gv_hbm, gf_hbm, gw_hbm,
    q_ref, k_ref, v_ref, gq_ref, gk_ref, gv_ref, gw_ref,
    G, S, W, ext, conv, ga, gg, filt, filt_ahead, filt_back, cotangent, gt_own, gt_sib,
    halo_s, halo_r, back_s, back_r,
    part, plus_s, plus_r, minus_s, minus_r, pair_s, pair_r,
    taps, taps_sib, taps_mine, taps_parts, taps_all,
    send, recv, part_send, part_recv, all_send, all_recv, in_sem, out_sem,
):
    ctx = lax.axis_index("ctx")
    t = lax.axis_index("tp")
    z = ctx // 4
    yh = lax.rem(ctx // 2, 2)
    core = lax.rem(ctx, 2)
    x = t // 2
    yl = lax.rem(t, 2)
    chip = ctx // 2

    def ctx_of(zz, hh, cc):
        return lax.rem(zz + 8, 8) * 4 + hh * 2 + cc

    def tp_of(xx, ll):
        return lax.rem(xx + 4, 4) * 2 + ll

    x_plus = (ctx, tp_of(x + 1, yl))
    x_minus = (ctx, tp_of(x - 1, yl))
    y_low = (ctx, tp_of(x, 1 - yl))
    z_plus = (ctx_of(z + 1, yh, core), t)
    z_minus = (ctx_of(z - 1, yh, core), t)
    y_high = (ctx_of(z, 1 - yh, core), t)
    sibling = (ctx_of(z, yh, 1 - core), t)
    after = (lax.rem(ctx + 1, 32), t)
    before = (lax.rem(ctx + 31, 32), t)
    beyond = (lax.rem(ctx + 31 + 2 * core, 32), t)

    def chip_device(other):
        return (other * 2 + core, t)

    started = []

    def push(src, dst, device):
        slot = len(started)
        copy = pltpu.make_async_remote_copy(
            src_ref=src, dst_ref=dst, send_sem=send.at[slot], recv_sem=recv.at[slot],
            device_id=device, device_id_type=MESH,
        )
        copy.start()
        started.append(copy)
        return copy

    barrier = pltpu.get_barrier_semaphore()
    for device in (x_plus, x_minus, y_low, z_plus, z_minus, y_high, sibling, beyond):
        pl.semaphore_signal(barrier, inc=1, device_id=device, device_id_type=MESH)

    loads = []

    def load(src, dst):
        copy = pltpu.make_async_copy(src, dst, in_sem.at[len(loads)])
        copy.start()
        loads.append(copy)

    for g in range(4):
        load(g_hbm.at[:, lanes(g)], G.at[t, g // 2, g % 2])
    load(w_hbm, W.at[ctx])
    load(k_hbm, k_ref)
    load(v_hbm, v_ref)
    for g in range(4):
        load(f_hbm.at[:, lanes(g)], filt.at[g])
    load(q_hbm, q_ref)

    stores = []

    def store(src, dst):
        copy = pltpu.make_async_copy(src, dst, out_sem.at[len(stores)])
        copy.start()
        stores.append(copy)

    for copy in loads[:5]:
        copy.wait()
    pl.semaphore_wait(barrier, 8)

    pieces = ((1 - yh, 256, 256, 48), (yh, 256, 256, 48), (1 - yh, 0, 256, 48), (yh, 0, 256, 48))
    b_minus, b_plus, b_far = tp_of(x - 1, yl), tp_of(x + 1, yl), tp_of(x + 2, yl)
    p_own, p_minus, p_plus, p_far = (
        tp_of(x, 1 - yl), tp_of(x - 1, 1 - yl), tp_of(x + 1, 1 - yl), tp_of(x + 2, 1 - yl)
    )
    flight = {}
    shared = {}

    def push_rows(p, j, start, size, device):
        hs, first = pieces[p][:2]
        ref = G.at[j, hs, :, pl.ds(first + start, size)]
        return push(ref, ref, device)

    def share_g(p, j):
        hs, first, count, edge = pieces[p]
        here = pl.ds(first, count)
        shared.setdefault(p, []).append(
            push(G.at[j, hs, 1 - core, here], S.at[j, hs, here], sibling)
        )

    def gather_0(p):
        count = pieces[p][2]
        flight[p, "plus"] = push_rows(p, t, 0, count, x_plus)
        flight[p, "minus"] = push_rows(p, t, 0, count, x_minus)
        flight[p, "low"] = push_rows(p, t, 0, count, y_low)
        share_g(p, t)

    def gather_1(p):
        hs, first, count, edge = pieces[p]
        half = count // 2
        flight[p, "low"].wait_recv()
        flight[p, "a_plus"] = push_rows(p, p_own, edge, count - 2 * edge, x_plus)
        flight[p, "a_minus"] = push_rows(p, p_own, edge, count - 2 * edge, x_minus)
        flight[p, "plus"].wait_recv()
        flight[p, "half_plus"] = push_rows(p, b_minus, 0, half, x_plus)
        flight[p, "low_0"] = push_rows(p, b_minus, 0, edge, y_low)
        flight[p, "low_1"] = push_rows(p, b_minus, count - edge, edge, y_low)
        flight[p, "minus"].wait_recv()
        flight[p, "half_minus"] = push_rows(p, b_plus, half, half, x_minus)
        flight[p, "low_2"] = push_rows(p, b_plus, 0, edge, y_low)
        flight[p, "low_3"] = push_rows(p, b_plus, count - edge, edge, y_low)
        share_g(p, p_own)
        share_g(p, b_minus)
        share_g(p, b_plus)

    def gather_2(p):
        hs, first, count, edge = pieces[p]
        half = count // 2
        flight[p, "a_plus"].wait_recv()
        flight[p, "far_plus"] = push_rows(p, p_minus, edge, half - edge, x_plus)
        flight[p, "a_minus"].wait_recv()
        flight[p, "far_minus"] = push_rows(p, p_plus, half, half - edge, x_minus)
        flight[p, "half_plus"].wait_recv()
        flight[p, "low_4"] = push_rows(p, b_far, 0, edge, y_low)
        flight[p, "half_minus"].wait_recv()
        flight[p, "low_5"] = push_rows(p, b_far, count - edge, edge, y_low)
        share_g(p, b_far)

    def gather_3(p):
        for name in ("low_0", "low_1"):
            flight[p, name].wait_recv()
        share_g(p, p_minus)
        for name in ("low_2", "low_3"):
            flight[p, name].wait_recv()
        share_g(p, p_plus)
        for name in ("far_plus", "far_minus", "low_4", "low_5"):
            flight[p, name].wait_recv()
        share_g(p, p_far)

    w_plus = {}
    w_minus = {}
    w_shared = []

    def share_w(slot):
        w_shared.append(push(W.at[slot], W.at[slot], sibling))

    def forward_w(step, b):
        hh = yh if b == 0 else 1 - yh
        if step == 0:
            w_high.wait_recv()
            slot = ctx_of(z, 1 - yh, core)
            w_plus[1, 1] = push(W.at[slot], W.at[slot], z_plus)
            w_minus[1, 1] = push(W.at[slot], W.at[slot], z_minus)
            share_w(slot)
            return
        w_plus[step, b].wait_recv()
        w_minus[step, b].wait_recv()
        low = ctx_of(z - step, hh, core)
        high = ctx_of(z + step, hh, core)
        if step < 3:
            w_plus[step + 1, b] = push(W.at[low], W.at[low], z_plus)
            w_minus[step + 1, b] = push(W.at[high], W.at[high], z_minus)
        elif step == 3:
            w_plus[4, b] = push(W.at[low, pl.ds(0, 64)], W.at[low, pl.ds(0, 64)], z_plus)
            w_minus[4, b] = push(W.at[high, pl.ds(64, 64)], W.at[high, pl.ds(64, 64)], z_minus)
        share_w(low)
        if step < 4:
            share_w(high)

    def split_filters():
        for g in range(4):
            by_8 = [filt[g, 8 * k : 8 * k + 8, :] for k in range(16)]
            for i, row in enumerate(split_taps(by_8[::-1], LEVELS)):
                filt_back[g, 8 * i : 8 * i + 8, :] = row
            for i, row in enumerate(split_taps(by_8, LEVELS)):
                filt_ahead[g, 8 * i : 8 * i + 8, :] = row

    def forward_taps(b, group, count):
        def one(g, carry):
            def residue(r, sums):
                return add_taps(
                    sums, ext[g, pl.ds(b * 128 + 8 - r, 248), :],
                    lambda i: jnp.broadcast_to(filt_back[g, pl.ds(8 * i + r, 1), :], (8, 128)),
                )

            for m, row in enumerate(join_sums(lax.fori_loop(0, 8, residue, no_sums()), LEVELS)):
                conv[g, pl.ds(b * 128 + 8 * m, 8), :] = row
            return carry

        lax.fori_loop(group, group + count, one, 0)

    def filter_taps(g, first_block):
        for n in range(2):
            start = (first_block + n) * 128
            by_8 = [ga[g, start + 8 * k : start + 8 * k + 8, :] for k in range(16)]
            for i, row in enumerate(split_taps(by_8, LEVELS)):
                cotangent[n, 8 * i : 8 * i + 8, :] = row

        def residue(r, carry):
            def block(n, sums):
                return add_taps(
                    sums, ext[g, pl.ds((first_block + n) * 128 + 8 - r, 248), :],
                    lambda i: cotangent[n, 8 * i : 8 * i + 8, :],
                )

            sums = join_sums(lax.fori_loop(0, 2, block, no_sums()), LEVELS)
            for k in range(16):
                row = jnp.sum(sums[15 - k], axis=0, keepdims=True)
                if first_block == 0:
                    row += taps[g, pl.ds(8 * k + r, 1), :]
                taps[g, pl.ds(8 * k + r, 1), :] = row
            return carry

        lax.fori_loop(0, 8, residue, 0)

    def adjoint_taps(b):
        def one(g, carry):
            def residue(r, sums):
                return add_taps(
                    sums, ga[g, pl.ds(b * 128 + r, 248), :],
                    lambda i: jnp.broadcast_to(filt_ahead[g, pl.ds(8 * i + r, 1), :], (8, 128)),
                )

            sums = join_sums(lax.fori_loop(0, 8, residue, no_sums()), LEVELS)
            side = pl.ds(pl.multiple_of(g * 128, 128), 128)
            for m in range(0, 16, 2):
                here = pl.ds(b * 128 + 8 * m, 16)
                grad = jnp.concatenate([sums[m], sums[m + 1]], axis=0)
                gk_ref[here, side] = (grad * v_ref[here, side].astype(F32)).astype(BF16)
                gv_ref[here, side] = (grad * k_ref[here, side].astype(F32)).astype(BF16)
            return carry

        lax.fori_loop(0, 4, one, 0)

    def terms(r, s):
        hs = 1 - yh if r == 0 else yh
        ahead = lax.rem(z + 4 - s, 8)
        behind = lax.rem(z + 4 + s, 8) if s else z
        mine = jnp.concatenate([G[ahead, hs, core], G[behind, hs, core]], axis=1)
        theirs = jnp.concatenate([S[ahead, hs], S[behind, hs]], axis=1)
        part[r, s] = jnp.dot(gt_own[...], mine, preferred_element_type=F32) + jnp.dot(
            gt_sib[...], theirs, preferred_element_type=F32
        )

    sent_plus = {}
    sent_minus = {}

    def send_plus(r, step, h):
        total = part[r, step - 1, pl.ds(256 * h, 256), :128]
        if (r, step - 1, h) in sent_plus:
            sent_plus[r, step - 1, h].wait_recv()
            total = total + plus_r[r, step - 2, h].astype(F32)
        plus_s[r, step - 1, h] = total.astype(BF16)
        sent_plus[r, step, h] = push(plus_s.at[r, step - 1, h], plus_r.at[r, step - 1, h], z_plus)

    def send_minus(r, step, h):
        columns = pl.ds(0 if step == 1 else 128, 128)
        total = part[r, step - 1, pl.ds(256 * h, 256), columns]
        if (r, step - 1, h) in sent_minus:
            sent_minus[r, step - 1, h].wait_recv()
            total = total + minus_r[r, step - 2, h].astype(F32)
        minus_s[r, step - 1, h] = total.astype(BF16)
        sent_minus[r, step, h] = push(
            minus_s.at[r, step - 1, h], minus_r.at[r, step - 1, h], z_minus
        )

    def reduce_start(r):
        terms(r, 0)
        send_plus(r, 1, 0)
        send_minus(r, 1, 1)
        terms(r, 1)
        send_plus(r, 2, 1)
        send_minus(r, 2, 0)
        terms(r, 2)
        terms(r, 3)

    def reduce_step(r, n):
        step, late = ((2, 1), (3, 0), (3, 1), (4, 0), (4, 1))[n]
        send_plus(r, step, 1 - late)
        send_minus(r, step, late)

    def reduced(r, h):
        sent_plus[r, 4, h].wait_recv()
        sent_minus[r, 4, h].wait_recv()
        return (
            part[r, 0, pl.ds(256 * h, 256), 128:]
            + plus_r[r, 3, h].astype(F32)
            + minus_r[r, 3, h].astype(F32)
        )

    def accumulate(first, count):
        here = pl.ds(first, count)
        for n in range(4):
            block = jnp.concatenate(
                [G[2 * n + i // 4, (i // 2) % 2, i % 2, here] for i in range(8)], axis=1
            )
            grad = jnp.dot(block, W[pl.ds(8 * n, 8)].reshape(1024, 512), preferred_element_type=F32)
            gg[here, :] = grad if n == 0 else gg[here, :] + grad

    def finish_rows(first, count):
        here = pl.ds(first, count)
        for g in range(4):
            grad = gg[here, lanes(g)]
            gq_ref[here, lanes(g)] = (grad * conv[g, here, :]).astype(BF16)
            ga[g, here, :] = grad * q_ref[here, lanes(g)].astype(F32)

    def gate(groups):
        for g in groups:
            gated = (q_ref[:, lanes(g)].astype(F32) * conv[g]).astype(BF16)
            gt_own[pl.ds(g * 128, 128), :] = gated.astype(F32).T.astype(BF16)

    half = pl.ds(2 * core, 2)
    other_half = pl.ds(2 - 2 * core, 2)

    def piece(ref, owner):
        return ref.at[:, pl.ds(pl.multiple_of(owner * 8, 8), 8), :]

    def part_copy(step):
        owner = lax.rem(chip + step, 16)
        return pltpu.make_async_remote_copy(
            src_ref=piece(taps_mine, owner), dst_ref=taps_parts.at[step],
            send_sem=part_send.at[step], recv_sem=part_recv.at[step],
            device_id=chip_device(owner), device_id_type=MESH,
        )

    def all_copy(step):
        return pltpu.make_async_remote_copy(
            src_ref=taps_parts.at[0], dst_ref=piece(taps_all.at[half], chip),
            send_sem=all_send.at[step], recv_sem=all_recv.at[step],
            device_id=chip_device(lax.rem(chip + step, 16)), device_id_type=MESH,
        )

    def loop(action):
        def body(step, carry):
            action(step)
            return carry

        lax.fori_loop(1, 16, body, 0)

    def greet_far():
        for away in range(8):
            for hh in range(2):
                if (away, hh) not in ((0, 0), (1, 0), (7, 0), (0, 1)):
                    far = ctx_of(lax.rem(z + away, 8), lax.rem(yh + hh, 2), core)
                    pl.semaphore_signal(
                        barrier, inc=1, device_id=(far, t), device_id_type=MESH
                    )

    gather_0(0)
    w_high = push(W.at[ctx], W.at[ctx], y_high)
    w_plus[1, 0] = push(W.at[ctx], W.at[ctx], z_plus)
    w_minus[1, 0] = push(W.at[ctx], W.at[ctx], z_minus)
    share_w(ctx)
    for copy in loads[5:]:
        copy.wait()
    split_filters()
    for g in range(4):
        product = (k_ref[:, lanes(g)].astype(F32) * v_ref[:, lanes(g)].astype(F32)).astype(BF16)
        halo_s[:, lanes(g)] = product[384:]
        ext[g, 128:] = product.astype(F32)
    halo = push(halo_s, halo_r, after)
    gather_0(1)
    forward_taps(1, 0, 4)
    forward_w(0, 1)
    gather_1(0)
    gather_0(2)
    forward_w(1, 0)
    forward_taps(2, 0, 4)
    gather_1(1)
    forward_taps(3, 0, 3)
    forward_w(1, 1)
    gather_2(0)
    gather_0(3)
    forward_taps(3, 3, 1)
    forward_w(2, 0)
    halo.wait_recv()
    for g in range(4):
        rim = halo_r[:, lanes(g)].astype(F32)
        ext[g, :128] = jnp.where(ctx == 0, 0.0, rim)
    gather_1(2)
    forward_taps(0, 0, 4)
    forward_w(2, 1)
    gate((0,))
    gather_2(1)
    gate((1,))
    forward_w(3, 0)
    gate((2,))
    gather_1(3)
    gate((3,))
    gt_copy = push(gt_own, gt_sib, sibling)
    gather_3(0)
    forward_w(3, 1)
    forward_w(4, 0)
    gather_2(2)
    forward_w(4, 1)
    gather_3(1)
    for copy in w_shared:
        copy.wait_recv()
    accumulate(256, 256)
    greet_far()
    finish_rows(256, 256)
    gather_2(3)
    filter_taps(0, 2)
    filter_taps(1, 2)
    gather_3(2)
    gt_copy.wait_recv()
    for p in (0, 2):
        for copy in shared[p]:
            copy.wait_recv()
    reduce_start(0)
    filter_taps(2, 2)
    gather_3(3)
    for p in (1, 3):
        for copy in shared[p]:
            copy.wait_recv()
    reduce_start(1)
    accumulate(0, 256)
    finish_rows(0, 256)
    store(gq_ref, gq_hbm)
    for g in range(4):
        back_s[:, lanes(g)] = ga[g, :128, :].astype(BF16)
    back = push(back_s, back_r, before)
    reduce_step(0, 0)
    filter_taps(3, 2)
    filter_taps(0, 0)
    reduce_step(1, 0)
    filter_taps(1, 0)
    reduce_step(0, 1)
    filter_taps(2, 0)
    reduce_step(1, 1)
    filter_taps(3, 0)
    tap_pair = push(taps.at[other_half], taps_sib, sibling)
    reduce_step(0, 2)
    adjoint_taps(2)
    tap_pair.wait_recv()
    taps_mine[...] = taps[half] + taps_sib[...]
    pl.semaphore_wait(barrier, 12)
    loop(lambda step: part_copy(step).start())
    reduce_step(1, 2)
    adjoint_taps(1)
    reduce_step(0, 3)
    loop(lambda step: part_copy(step).wait_recv())
    mine = pl.ds(pl.multiple_of(chip * 8, 8), 8)
    total = taps_mine[:, mine, :]
    for step in range(1, 16):
        total = total + taps_parts[step]
    taps_parts[0] = total
    taps_all[half, mine, :] = total
    loop(lambda step: all_copy(step).start())
    reduce_step(1, 3)
    adjoint_taps(0)
    reduce_step(0, 4)
    reduce_step(1, 4)
    back.wait_recv()
    for g in range(4):
        rim = back_r[:, lanes(g)].astype(F32)
        ga[g, 512:] = jnp.where(ctx == 31, 0.0, rim)
    loop(lambda step: all_copy(step).wait_recv())
    spread = push(taps_all.at[half], taps_all.at[half], sibling)
    for h in range(2):
        pair_s[pl.ds(256 * h, 256), :] = reduced(0, h).astype(BF16)
    pair = push(pair_s, pair_r, y_high)
    adjoint_taps(3)
    store(gk_ref, gk_hbm)
    store(gv_ref, gv_hbm)
    spread.wait_recv()
    for g in range(4):
        store(taps_all.at[g], gf_hbm.at[:, lanes(g)])
    totals = [reduced(1, h) for h in range(2)]
    pair.wait_recv()
    for h in range(2):
        rows = pl.ds(256 * h, 256)
        gw_ref[:, rows] = (totals[h] + pair_r[rows, :].astype(F32)).T.astype(BF16)
    store(gw_ref, gw_hbm)
    for copy in started:
        copy.wait_send()
    loop(lambda step: part_copy(step).wait_send())
    loop(lambda step: all_copy(step).wait_send())
    for copy in stores:
        copy.wait()


def hand_on(*refs):
    sems = refs[10]
    copies = [pltpu.make_async_copy(refs[i], refs[5 + i], sems.at[i]) for i in range(5)]
    for copy in copies:
        copy.start()
    for copy in copies:
        copy.wait()


def local(query_act, key_act, value_act, filters, out_weight, grad_out):
    hbm = pl.BlockSpec(memory_space=pl.ANY)
    shape = jax.ShapeDtypeStruct
    tokens = shape((512, 512), BF16)
    block = pltpu.VMEM((512, 512), BF16)
    rim = pltpu.VMEM((128, 512), BF16)
    sums = pltpu.VMEM((2, 4, 2, 256, 128), BF16)
    results = pl.pallas_call(
        kernel,
        out_shape=(tokens, tokens, tokens, shape((128, 512), F32), shape((128, 512), BF16)),
        in_specs=[hbm] * 6,
        out_specs=(hbm,) * 5,
        scratch_shapes=[
            block, block, block, block, block, block, rim,
            pltpu.VMEM((8, 2, 2, 512, 128), BF16),
            pltpu.VMEM((8, 2, 512, 128), BF16),
            pltpu.VMEM((32, 128, 512), BF16),
            pltpu.VMEM((4, 640, 128), F32),
            pltpu.VMEM((4, 512, 128), F32),
            pltpu.VMEM((4, 640, 128), F32),
            pltpu.VMEM((512, 512), F32),
            pltpu.VMEM((4, 128, 128), F32),
            pltpu.VMEM((4, 8 * SUMS, 128), F32),
            pltpu.VMEM((4, 8 * SUMS, 128), F32),
            pltpu.VMEM((2, 8 * SUMS, 128), F32),
            block, block,
            rim, rim, rim, rim,
            pltpu.VMEM((2, 4, 512, 256), F32),
            sums, sums, sums, sums,
            pltpu.VMEM((512, 128), BF16),
            pltpu.VMEM((512, 128), BF16),
            pltpu.VMEM((4, 128, 128), F32),
            pltpu.VMEM((2, 128, 128), F32),
            pltpu.VMEM((2, 128, 128), F32),
            pltpu.VMEM((16, 2, 8, 128), F32),
            pltpu.VMEM((4, 128, 128), F32),
            pltpu.SemaphoreType.DMA((170,)),
            pltpu.SemaphoreType.DMA((170,)),
            pltpu.SemaphoreType.DMA((16,)),
            pltpu.SemaphoreType.DMA((16,)),
            pltpu.SemaphoreType.DMA((16,)),
            pltpu.SemaphoreType.DMA((16,)),
            pltpu.SemaphoreType.DMA((12,)),
            pltpu.SemaphoreType.DMA((8,)),
        ],
        compiler_params=pltpu.CompilerParams(
            collective_id=0, has_side_effects=True, vmem_limit_bytes=60 * 2**20
        ),
        cost_estimate=pl.CostEstimate(flops=4 * 10**9, bytes_accessed=5 * 2**20, transcendentals=0),
        name="block_grads",
    )(query_act, key_act, value_act, filters, out_weight, grad_out)
    return pl.pallas_call(
        hand_on,
        out_shape=(tokens, tokens, tokens, shape((128, 512), F32), shape((128, 512), BF16)),
        in_specs=[pl.BlockSpec(memory_space=pltpu.VMEM)] * 5,
        out_specs=(hbm,) * 5,
        scratch_shapes=[pltpu.SemaphoreType.DMA((5,))],
        name="hand_on",
    )(*results)


def solution(mesh):
    placed = (
        P("ctx", "tp"),
        P("ctx", "tp"),
        P("ctx", "tp"),
        P(None, "tp"),
        P("ctx", "tp"),
        P("ctx", "tp"),
    )
    return jax.shard_map(
        local,
        mesh=mesh,
        in_specs=placed,
        out_specs=(P("ctx", "tp"), P("ctx", "tp"), P("ctx", "tp"), P(None, "tp"), P("ctx", "tp")),
        check_vma=False,
    )
```

```python
import jax
import jax.numpy as jnp
from jax import lax
from jax.experimental import pallas as pl
from jax.experimental.pallas import tpu as pltpu
from jax.sharding import PartitionSpec as P

MESH = pl.DeviceIdType.MESH
BF16 = jnp.bfloat16
F32 = jnp.float32


def lanes(group):
    return pl.ds(group * 128, 128)


LEVELS = 2
LEAF = 16 >> LEVELS
SUMS = 3**LEVELS * LEAF


def split_taps(taps, levels):
    if levels == 0:
        return list(taps)
    even, odd = taps[0::2], taps[1::2]
    both = [a + b for a, b in zip(even, odd)]
    return (
        split_taps(both, levels - 1) + split_taps(even, levels - 1) + split_taps(odd, levels - 1)
    )


def split_rows(rows, levels):
    if levels == 0:
        return [rows]
    even, odd = rows[0::2], rows[1::2]
    here = [a - b for a, b in zip(even[:-1], odd)]
    moved = [a - b for a, b in zip(even[1:], odd)]
    return (
        split_rows(odd, levels - 1) + split_rows(here, levels - 1) + split_rows(moved, levels - 1)
    )


def join_sums(sums, levels):
    if levels == 0:
        return list(sums)
    third = len(sums) // 3
    both, even, odd = (
        join_sums(sums[i * third : (i + 1) * third], levels - 1) for i in range(3)
    )
    joined = []
    for p, a, b in zip(both, even, odd):
        joined += [p + a, p + b]
    return joined


def add_taps(sums, window, tap):
    vectors = [window[8 * i : 8 * i + 8] for i in range(31)]
    result = []
    for leaf, rows in enumerate(split_rows(vectors, LEVELS)):
        taps = [tap(leaf * LEAF + k) for k in range(LEAF)]
        for m in range(LEAF):
            total = sums[leaf * LEAF + m]
            for k in range(LEAF):
                total = total + taps[k] * rows[m + k]
            result.append(total)
    return tuple(result)


def no_sums():
    return tuple(jnp.zeros((8, 128), F32) for _ in range(SUMS))


def kernel(
    q_hbm, k_hbm, v_hbm, f_hbm, w_hbm, g_hbm,
    gq_hbm, gk_hbm, gv_hbm, gf_hbm, gw_hbm,
    q_ref, k_ref, v_ref, gq_ref, gk_ref, gv_ref, gw_ref,
    G, S, W, ext, conv, ga, gg, filt, filt_ahead, filt_back, cotangent, gt_own, gt_sib,
    halo_s, halo_r, back_s, back_r,
    part, plus_s, plus_r, minus_s, minus_r, pair_s, pair_r,
    taps, taps_sib, taps_mine, taps_parts, taps_all,
    send, recv, part_send, part_recv, all_send, all_recv, in_sem, out_sem,
):
    ctx = lax.axis_index("ctx")
    t = lax.axis_index("tp")
    z = ctx // 4
    yh = lax.rem(ctx // 2, 2)
    core = lax.rem(ctx, 2)
    x = t // 2
    yl = lax.rem(t, 2)
    chip = ctx // 2

    def ctx_of(zz, hh, cc):
        return lax.rem(zz + 8, 8) * 4 + hh * 2 + cc

    def tp_of(xx, ll):
        return lax.rem(xx + 4, 4) * 2 + ll

    x_plus = (ctx, tp_of(x + 1, yl))
    x_minus = (ctx, tp_of(x - 1, yl))
    y_low = (ctx, tp_of(x, 1 - yl))
    z_plus = (ctx_of(z + 1, yh, core), t)
    z_minus = (ctx_of(z - 1, yh, core), t)
    y_high = (ctx_of(z, 1 - yh, core), t)
    sibling = (ctx_of(z, yh, 1 - core), t)
    after = (lax.rem(ctx + 1, 32), t)
    before = (lax.rem(ctx + 31, 32), t)
    beyond = (lax.rem(ctx + 31 + 2 * core, 32), t)

    def chip_device(other):
        return (other * 2 + core, t)

    started = []

    def push(src, dst, device):
        slot = len(started)
        copy = pltpu.make_async_remote_copy(
            src_ref=src, dst_ref=dst, send_sem=send.at[slot], recv_sem=recv.at[slot],
            device_id=device, device_id_type=MESH,
        )
        copy.start()
        started.append(copy)
        return copy

    barrier = pltpu.get_barrier_semaphore()
    for device in (x_plus, x_minus, y_low, z_plus, z_minus, y_high, sibling, beyond):
        pl.semaphore_signal(barrier, inc=1, device_id=device, device_id_type=MESH)

    loads = []

    def load(src, dst):
        copy = pltpu.make_async_copy(src, dst, in_sem.at[len(loads)])
        copy.start()
        loads.append(copy)

    for g in range(4):
        load(g_hbm.at[:, lanes(g)], G.at[t, g // 2, g % 2])
    load(w_hbm, W.at[ctx])
    load(k_hbm, k_ref)
    load(v_hbm, v_ref)
    for g in range(4):
        load(f_hbm.at[:, lanes(g)], filt.at[g])
    load(q_hbm, q_ref)

    stores = []

    def store(src, dst):
        copy = pltpu.make_async_copy(src, dst, out_sem.at[len(stores)])
        copy.start()
        stores.append(copy)

    for copy in loads[:5]:
        copy.wait()
    pl.semaphore_wait(barrier, 8)

    pieces = ((1 - yh, 256, 256, 48), (yh, 256, 256, 48), (1 - yh, 0, 256, 48), (yh, 0, 256, 48))
    b_minus, b_plus, b_far = tp_of(x - 1, yl), tp_of(x + 1, yl), tp_of(x + 2, yl)
    p_own, p_minus, p_plus, p_far = (
        tp_of(x, 1 - yl), tp_of(x - 1, 1 - yl), tp_of(x + 1, 1 - yl), tp_of(x + 2, 1 - yl)
    )
    flight = {}
    shared = {}

    def push_rows(p, j, start, size, device):
        hs, first = pieces[p][:2]
        ref = G.at[j, hs, :, pl.ds(first + start, size)]
        return push(ref, ref, device)

    def share_g(p, j):
        hs, first, count, edge = pieces[p]
        here = pl.ds(first, count)
        shared.setdefault(p, []).append(
            push(G.at[j, hs, 1 - core, here], S.at[j, hs, here], sibling)
        )

    def gather_0(p):
        count = pieces[p][2]
        flight[p, "plus"] = push_rows(p, t, 0, count, x_plus)
        flight[p, "minus"] = push_rows(p, t, 0, count, x_minus)
        flight[p, "low"] = push_rows(p, t, 0, count, y_low)
        share_g(p, t)

    def gather_1(p):
        hs, first, count, edge = pieces[p]
        half = count // 2
        flight[p, "low"].wait_recv()
        flight[p, "a_plus"] = push_rows(p, p_own, edge, count - 2 * edge, x_plus)
        flight[p, "a_minus"] = push_rows(p, p_own, edge, count - 2 * edge, x_minus)
        flight[p, "plus"].wait_recv()
        flight[p, "half_plus"] = push_rows(p, b_minus, 0, half, x_plus)
        flight[p, "low_0"] = push_rows(p, b_minus, 0, edge, y_low)
        flight[p, "low_1"] = push_rows(p, b_minus, count - edge, edge, y_low)
        flight[p, "minus"].wait_recv()
        flight[p, "half_minus"] = push_rows(p, b_plus, half, half, x_minus)
        flight[p, "low_2"] = push_rows(p, b_plus, 0, edge, y_low)
        flight[p, "low_3"] = push_rows(p, b_plus, count - edge, edge, y_low)
        share_g(p, p_own)
        share_g(p, b_minus)
        share_g(p, b_plus)

    def gather_2(p):
        hs, first, count, edge = pieces[p]
        half = count // 2
        flight[p, "a_plus"].wait_recv()
        flight[p, "far_plus"] = push_rows(p, p_minus, edge, half - edge, x_plus)
        flight[p, "a_minus"].wait_recv()
        flight[p, "far_minus"] = push_rows(p, p_plus, half, half - edge, x_minus)
        flight[p, "half_plus"].wait_recv()
        flight[p, "low_4"] = push_rows(p, b_far, 0, edge, y_low)
        flight[p, "half_minus"].wait_recv()
        flight[p, "low_5"] = push_rows(p, b_far, count - edge, edge, y_low)
        share_g(p, b_far)

    def gather_3(p):
        for name in ("low_0", "low_1"):
            flight[p, name].wait_recv()
        share_g(p, p_minus)
        for name in ("low_2", "low_3"):
            flight[p, name].wait_recv()
        share_g(p, p_plus)
        for name in ("far_plus", "far_minus", "low_4", "low_5"):
            flight[p, name].wait_recv()
        share_g(p, p_far)

    w_plus = {}
    w_minus = {}
    w_shared = []

    def share_w(slot):
        w_shared.append(push(W.at[slot], W.at[slot], sibling))

    def forward_w(step, b):
        hh = yh if b == 0 else 1 - yh
        if step == 0:
            w_high.wait_recv()
            slot = ctx_of(z, 1 - yh, core)
            w_plus[1, 1] = push(W.at[slot], W.at[slot], z_plus)
            w_minus[1, 1] = push(W.at[slot], W.at[slot], z_minus)
            share_w(slot)
            return
        w_plus[step, b].wait_recv()
        w_minus[step, b].wait_recv()
        low = ctx_of(z - step, hh, core)
        high = ctx_of(z + step, hh, core)
        if step < 3:
            w_plus[step + 1, b] = push(W.at[low], W.at[low], z_plus)
            w_minus[step + 1, b] = push(W.at[high], W.at[high], z_minus)
        elif step == 3:
            w_plus[4, b] = push(W.at[low, pl.ds(0, 64)], W.at[low, pl.ds(0, 64)], z_plus)
            w_minus[4, b] = push(W.at[high, pl.ds(64, 64)], W.at[high, pl.ds(64, 64)], z_minus)
        share_w(low)
        if step < 4:
            share_w(high)

    def split_filters():
        for g in range(4):
            by_8 = [filt[g, 8 * k : 8 * k + 8, :] for k in range(16)]
            for i, row in enumerate(split_taps(by_8[::-1], LEVELS)):
                filt_back[g, 8 * i : 8 * i + 8, :] = row
            for i, row in enumerate(split_taps(by_8, LEVELS)):
                filt_ahead[g, 8 * i : 8 * i + 8, :] = row

    def forward_taps(b, group, count):
        def one(g, carry):
            def residue(r, sums):
                return add_taps(
                    sums, ext[g, pl.ds(b * 128 + 8 - r, 248), :],
                    lambda i: jnp.broadcast_to(filt_back[g, pl.ds(8 * i + r, 1), :], (8, 128)),
                )

            for m, row in enumerate(join_sums(lax.fori_loop(0, 8, residue, no_sums()), LEVELS)):
                conv[g, pl.ds(b * 128 + 8 * m, 8), :] = row
            return carry

        lax.fori_loop(group, group + count, one, 0)

    def filter_taps(g, first_block):
        for n in range(2):
            start = (first_block + n) * 128
            by_8 = [ga[g, start + 8 * k : start + 8 * k + 8, :] for k in range(16)]
            for i, row in enumerate(split_taps(by_8, LEVELS)):
                cotangent[n, 8 * i : 8 * i + 8, :] = row

        def residue(r, carry):
            def block(n, sums):
                return add_taps(
                    sums, ext[g, pl.ds((first_block + n) * 128 + 8 - r, 248), :],
                    lambda i: cotangent[n, 8 * i : 8 * i + 8, :],
                )

            sums = join_sums(lax.fori_loop(0, 2, block, no_sums()), LEVELS)
            for k in range(16):
                row = jnp.sum(sums[15 - k], axis=0, keepdims=True)
                if first_block == 0:
                    row += taps[g, pl.ds(8 * k + r, 1), :]
                taps[g, pl.ds(8 * k + r, 1), :] = row
            return carry

        lax.fori_loop(0, 8, residue, 0)

    def adjoint_taps(b):
        def one(g, carry):
            def residue(r, sums):
                return add_taps(
                    sums, ga[g, pl.ds(b * 128 + r, 248), :],
                    lambda i: jnp.broadcast_to(filt_ahead[g, pl.ds(8 * i + r, 1), :], (8, 128)),
                )

            sums = join_sums(lax.fori_loop(0, 8, residue, no_sums()), LEVELS)
            side = pl.ds(pl.multiple_of(g * 128, 128), 128)
            for m in range(0, 16, 2):
                here = pl.ds(b * 128 + 8 * m, 16)
                grad = jnp.concatenate([sums[m], sums[m + 1]], axis=0)
                gk_ref[here, side] = (grad * v_ref[here, side].astype(F32)).astype(BF16)
                gv_ref[here, side] = (grad * k_ref[here, side].astype(F32)).astype(BF16)
            return carry

        lax.fori_loop(0, 4, one, 0)

    def terms(r, s):
        hs = 1 - yh if r == 0 else yh
        ahead = lax.rem(z + 4 - s, 8)
        behind = lax.rem(z + 4 + s, 8) if s else z
        mine = jnp.concatenate([G[ahead, hs, core], G[behind, hs, core]], axis=1)
        theirs = jnp.concatenate([S[ahead, hs], S[behind, hs]], axis=1)
        part[r, s] = jnp.dot(gt_own[...], mine, preferred_element_type=F32) + jnp.dot(
            gt_sib[...], theirs, preferred_element_type=F32
        )

    sent_plus = {}
    sent_minus = {}

    def send_plus(r, step, h):
        total = part[r, step - 1, pl.ds(256 * h, 256), :128]
        if (r, step - 1, h) in sent_plus:
            sent_plus[r, step - 1, h].wait_recv()
            total = total + plus_r[r, step - 2, h].astype(F32)
        plus_s[r, step - 1, h] = total.astype(BF16)
        sent_plus[r, step, h] = push(plus_s.at[r, step - 1, h], plus_r.at[r, step - 1, h], z_plus)

    def send_minus(r, step, h):
        columns = pl.ds(0 if step == 1 else 128, 128)
        total = part[r, step - 1, pl.ds(256 * h, 256), columns]
        if (r, step - 1, h) in sent_minus:
            sent_minus[r, step - 1, h].wait_recv()
            total = total + minus_r[r, step - 2, h].astype(F32)
        minus_s[r, step - 1, h] = total.astype(BF16)
        sent_minus[r, step, h] = push(
            minus_s.at[r, step - 1, h], minus_r.at[r, step - 1, h], z_minus
        )

    def reduce_start(r):
        terms(r, 0)
        send_plus(r, 1, 0)
        send_minus(r, 1, 1)
        terms(r, 1)
        send_plus(r, 2, 1)
        send_minus(r, 2, 0)
        terms(r, 2)
        terms(r, 3)

    def reduce_step(r, n):
        step, late = ((2, 1), (3, 0), (3, 1), (4, 0), (4, 1))[n]
        send_plus(r, step, 1 - late)
        send_minus(r, step, late)

    def reduced(r, h):
        sent_plus[r, 4, h].wait_recv()
        sent_minus[r, 4, h].wait_recv()
        return (
            part[r, 0, pl.ds(256 * h, 256), 128:]
            + plus_r[r, 3, h].astype(F32)
            + minus_r[r, 3, h].astype(F32)
        )

    def accumulate(first, count):
        here = pl.ds(first, count)
        for n in range(4):
            block = jnp.concatenate(
                [G[2 * n + i // 4, (i // 2) % 2, i % 2, here] for i in range(8)], axis=1
            )
            grad = jnp.dot(block, W[pl.ds(8 * n, 8)].reshape(1024, 512), preferred_element_type=F32)
            gg[here, :] = grad if n == 0 else gg[here, :] + grad

    def finish_rows(first, count):
        here = pl.ds(first, count)
        for g in range(4):
            grad = gg[here, lanes(g)]
            gq_ref[here, lanes(g)] = (grad * conv[g, here, :]).astype(BF16)
            ga[g, here, :] = grad * q_ref[here, lanes(g)].astype(F32)

    def gate(groups):
        for g in groups:
            gated = (q_ref[:, lanes(g)].astype(F32) * conv[g]).astype(BF16)
            gt_own[pl.ds(g * 128, 128), :] = gated.astype(F32).T.astype(BF16)

    half = pl.ds(2 * core, 2)
    other_half = pl.ds(2 - 2 * core, 2)

    def piece(ref, owner):
        return ref.at[:, pl.ds(pl.multiple_of(owner * 8, 8), 8), :]

    def part_copy(step):
        owner = lax.rem(chip + step, 16)
        return pltpu.make_async_remote_copy(
            src_ref=piece(taps_mine, owner), dst_ref=taps_parts.at[step],
            send_sem=part_send.at[step], recv_sem=part_recv.at[step],
            device_id=chip_device(owner), device_id_type=MESH,
        )

    def all_copy(step):
        return pltpu.make_async_remote_copy(
            src_ref=taps_parts.at[0], dst_ref=piece(taps_all.at[half], chip),
            send_sem=all_send.at[step], recv_sem=all_recv.at[step],
            device_id=chip_device(lax.rem(chip + step, 16)), device_id_type=MESH,
        )

    def loop(action):
        def body(step, carry):
            action(step)
            return carry

        lax.fori_loop(1, 16, body, 0)

    def greet_far():
        for away in range(8):
            for hh in range(2):
                if (away, hh) not in ((0, 0), (1, 0), (7, 0), (0, 1)):
                    far = ctx_of(lax.rem(z + away, 8), lax.rem(yh + hh, 2), core)
                    pl.semaphore_signal(
                        barrier, inc=1, device_id=(far, t), device_id_type=MESH
                    )

    gather_0(0)
    w_high = push(W.at[ctx], W.at[ctx], y_high)
    w_plus[1, 0] = push(W.at[ctx], W.at[ctx], z_plus)
    w_minus[1, 0] = push(W.at[ctx], W.at[ctx], z_minus)
    share_w(ctx)
    for copy in loads[5:]:
        copy.wait()
    split_filters()
    for g in range(4):
        product = (k_ref[:, lanes(g)].astype(F32) * v_ref[:, lanes(g)].astype(F32)).astype(BF16)
        halo_s[:, lanes(g)] = product[384:]
        ext[g, 128:] = product.astype(F32)
    halo = push(halo_s, halo_r, after)
    gather_0(1)
    forward_taps(1, 0, 4)
    forward_w(0, 1)
    gather_1(0)
    gather_0(2)
    forward_w(1, 0)
    forward_taps(2, 0, 4)
    gather_1(1)
    forward_taps(3, 0, 3)
    forward_w(1, 1)
    gather_2(0)
    gather_0(3)
    forward_taps(3, 3, 1)
    forward_w(2, 0)
    halo.wait_recv()
    for g in range(4):
        rim = halo_r[:, lanes(g)].astype(F32)
        ext[g, :128] = jnp.where(ctx == 0, 0.0, rim)
    gather_1(2)
    forward_taps(0, 0, 4)
    forward_w(2, 1)
    gate((0,))
    gather_2(1)
    gate((1,))
    forward_w(3, 0)
    gate((2,))
    gather_1(3)
    gate((3,))
    gt_copy = push(gt_own, gt_sib, sibling)
    gather_3(0)
    forward_w(3, 1)
    forward_w(4, 0)
    gather_2(2)
    forward_w(4, 1)
    gather_3(1)
    for copy in w_shared:
        copy.wait_recv()
    accumulate(256, 256)
    greet_far()
    finish_rows(256, 256)
    gather_2(3)
    filter_taps(0, 2)
    filter_taps(1, 2)
    gather_3(2)
    gt_copy.wait_recv()
    for p in (0, 2):
        for copy in shared[p]:
            copy.wait_recv()
    reduce_start(0)
    filter_taps(2, 2)
    gather_3(3)
    for p in (1, 3):
        for copy in shared[p]:
            copy.wait_recv()
    reduce_start(1)
    accumulate(0, 256)
    finish_rows(0, 256)
    store(gq_ref, gq_hbm)
    for g in range(4):
        back_s[:, lanes(g)] = ga[g, :128, :].astype(BF16)
    back = push(back_s, back_r, before)
    reduce_step(0, 0)
    filter_taps(3, 2)
    filter_taps(0, 0)
    reduce_step(1, 0)
    filter_taps(1, 0)
    reduce_step(0, 1)
    filter_taps(2, 0)
    reduce_step(1, 1)
    filter_taps(3, 0)
    tap_pair = push(taps.at[other_half], taps_sib, sibling)
    reduce_step(0, 2)
    adjoint_taps(2)
    tap_pair.wait_recv()
    taps_mine[...] = taps[half] + taps_sib[...]
    pl.semaphore_wait(barrier, 12)
    loop(lambda step: part_copy(step).start())
    reduce_step(1, 2)
    adjoint_taps(1)
    reduce_step(0, 3)
    loop(lambda step: part_copy(step).wait_recv())
    mine = pl.ds(pl.multiple_of(chip * 8, 8), 8)
    total = taps_mine[:, mine, :]
    for step in range(1, 16):
        total = total + taps_parts[step]
    taps_parts[0] = total
    taps_all[half, mine, :] = total
    loop(lambda step: all_copy(step).start())
    reduce_step(1, 3)
    adjoint_taps(0)
    reduce_step(0, 4)
    reduce_step(1, 4)
    back.wait_recv()
    for g in range(4):
        rim = back_r[:, lanes(g)].astype(F32)
        ga[g, 512:] = jnp.where(ctx == 31, 0.0, rim)
    loop(lambda step: all_copy(step).wait_recv())
    spread = push(taps_all.at[half], taps_all.at[half], sibling)
    for h in range(2):
        pair_s[pl.ds(256 * h, 256), :] = reduced(0, h).astype(BF16)
    pair = push(pair_s, pair_r, y_high)
    adjoint_taps(3)
    store(gk_ref, gk_hbm)
    store(gv_ref, gv_hbm)
    spread.wait_recv()
    for g in range(4):
        store(taps_all.at[g], gf_hbm.at[:, lanes(g)])
    totals = [reduced(1, h) for h in range(2)]
    pair.wait_recv()
    for h in range(2):
        rows = pl.ds(256 * h, 256)
        gw_ref[:, rows] = (totals[h] + pair_r[rows, :].astype(F32)).T.astype(BF16)
    store(gw_ref, gw_hbm)
    for copy in started:
        copy.wait_send()
    loop(lambda step: part_copy(step).wait_send())
    loop(lambda step: all_copy(step).wait_send())
    for copy in stores:
        copy.wait()


def hand_on(*refs):
    held, arrived, left = refs[10:15], refs[15], refs[16]
    loads = [pltpu.make_async_copy(refs[i], held[i], arrived.at[i]) for i in range(5)]
    stores = [pltpu.make_async_copy(held[i], refs[5 + i], left.at[i]) for i in range(5)]
    for copy in loads:
        copy.start()
    for i in range(5):
        loads[i].wait()
        stores[i].start()
    for copy in stores:
        copy.wait()


def local(query_act, key_act, value_act, filters, out_weight, grad_out):
    hbm = pl.BlockSpec(memory_space=pl.ANY)
    shape = jax.ShapeDtypeStruct
    tokens = shape((512, 512), BF16)
    block = pltpu.VMEM((512, 512), BF16)
    rim = pltpu.VMEM((128, 512), BF16)
    sums = pltpu.VMEM((2, 4, 2, 256, 128), BF16)
    results = pl.pallas_call(
        kernel,
        out_shape=(tokens, tokens, tokens, shape((128, 512), F32), shape((128, 512), BF16)),
        in_specs=[hbm] * 6,
        out_specs=(hbm,) * 5,
        scratch_shapes=[
            block, block, block, block, block, block, rim,
            pltpu.VMEM((8, 2, 2, 512, 128), BF16),
            pltpu.VMEM((8, 2, 512, 128), BF16),
            pltpu.VMEM((32, 128, 512), BF16),
            pltpu.VMEM((4, 640, 128), F32),
            pltpu.VMEM((4, 512, 128), F32),
            pltpu.VMEM((4, 640, 128), F32),
            pltpu.VMEM((512, 512), F32),
            pltpu.VMEM((4, 128, 128), F32),
            pltpu.VMEM((4, 8 * SUMS, 128), F32),
            pltpu.VMEM((4, 8 * SUMS, 128), F32),
            pltpu.VMEM((2, 8 * SUMS, 128), F32),
            block, block,
            rim, rim, rim, rim,
            pltpu.VMEM((2, 4, 512, 256), F32),
            sums, sums, sums, sums,
            pltpu.VMEM((512, 128), BF16),
            pltpu.VMEM((512, 128), BF16),
            pltpu.VMEM((4, 128, 128), F32),
            pltpu.VMEM((2, 128, 128), F32),
            pltpu.VMEM((2, 128, 128), F32),
            pltpu.VMEM((16, 2, 8, 128), F32),
            pltpu.VMEM((4, 128, 128), F32),
            pltpu.SemaphoreType.DMA((170,)),
            pltpu.SemaphoreType.DMA((170,)),
            pltpu.SemaphoreType.DMA((16,)),
            pltpu.SemaphoreType.DMA((16,)),
            pltpu.SemaphoreType.DMA((16,)),
            pltpu.SemaphoreType.DMA((16,)),
            pltpu.SemaphoreType.DMA((12,)),
            pltpu.SemaphoreType.DMA((8,)),
        ],
        compiler_params=pltpu.CompilerParams(
            collective_id=0, has_side_effects=True, vmem_limit_bytes=60 * 2**20
        ),
        cost_estimate=pl.CostEstimate(flops=4 * 10**9, bytes_accessed=5 * 2**20, transcendentals=0),
        name="block_grads",
    )(query_act, key_act, value_act, filters, out_weight, grad_out)
    return pl.pallas_call(
        hand_on,
        out_shape=(tokens, tokens, tokens, shape((128, 512), F32), shape((128, 512), BF16)),
        in_specs=[hbm] * 5,
        out_specs=(hbm,) * 5,
        scratch_shapes=[
            block, block, block,
            pltpu.VMEM((128, 512), F32),
            rim,
            pltpu.SemaphoreType.DMA((5,)),
            pltpu.SemaphoreType.DMA((5,)),
        ],
        name="hand_on",
    )(*results)


def solution(mesh):
    placed = (
        P("ctx", "tp"),
        P("ctx", "tp"),
        P("ctx", "tp"),
        P(None, "tp"),
        P("ctx", "tp"),
        P("ctx", "tp"),
    )
    return jax.shard_map(
        local,
        mesh=mesh,
        in_specs=placed,
        out_specs=(P("ctx", "tp"), P("ctx", "tp"), P("ctx", "tp"), P(None, "tp"), P("ctx", "tp")),
        check_vma=False,
    )
```
